32 devices in a mesh: groups: 2 (over y), ctx: 4 (over z), dp: 4 (over x, core).
Axes of the slice: x: 2, y: 2, z: 4, core: 2. Of those that a mesh axis runs over, the one named last changes fastest.
Arguments:
- layer_input: bfloat16 [8, 512, 4096], P(('groups', 'dp'), 'ctx'), parts along dimension 0, may hold values from -6 to 6
- head_input: bfloat16 [8, 512, 2048], P(('groups', 'dp'), 'ctx'), parts along dimension 0, may hold values from -6 to 6
- input_map: bfloat16 [8, 512, 64], P(('groups', 'dp'), 'ctx'), parts along dimension 0, may hold values from -2 to 2
- output_map: bfloat16 [8, 512, 64], P(('groups', 'dp'), 'ctx'), parts along dimension 0, may hold values from -0.25 to 0.25
- step_weight: bfloat16 [4096, 64], P(('ctx', 'dp')), may hold values from -0.09375 to 0.09375
- decay_log: float32 [64], replicated, may hold values from -9 to -3
- pack_place: int32 [8, 512], P(('groups', 'dp')), parts along dimension 0, may hold values from 0 to 511, as said below
- doc_starts: int32 [8, 512], P(('groups', 'dp'), 'ctx'), parts along dimension 0, may hold values from 0 to 1, as said below
- out_grad: bfloat16 [8, 512, 2048], P(('groups', 'dp'), 'ctx'), parts along dimension 0, may hold values from -1.5 to 1.5
Outputs:
- head_input_grad: bfloat16 [8, 512, 2048], P(('groups', 'dp'), 'ctx'), parts along dimension 0
- input_map_grad: float32 [8, 512, 64], P(('groups', 'dp'), 'ctx'), parts along dimension 0
- output_map_grad: float32 [8, 512, 64], P(('groups', 'dp'), 'ctx'), parts along dimension 0
- step_weight_grad: float32 [8192, 64], P(('groups', 'ctx', 'dp')), parts along dimension 0
The draws below stay inside these ranges and needn't reach their ends.
There are 2 independent parts, one for each index of `groups`. The reference program is written for one: setup_inputs(seed, part) draws one part's arguments, and reference() takes and returns one part's arrays. A program takes and returns all parts, laid end to end along the dimension named above; an argument that names none is the same for every part. Nothing has to cross between parts.
Inputs may be any that keep to these rules, and one draw needn't show every extreme that they name: `pack_place`: each row is a permutation of the packed positions; of the 128 tokens at sampler positions k * 128 to (k + 1) * 128 - 1, exactly 32 land in each block of 128 packed positions. `doc_starts`: the first position of every row is 1.
All inputs are finite; a program needn't handle non-finite values.
Results may differ from the reference program's by a relative error of at most 0.0038.
Values may be sent and summed in bfloat16 or wider, within the bound.
A program may use at most 128 MiB of HBM per device.

```python
import jax
import jax.numpy as jnp
from jax import lax

D = 4096
H = 64
P_SIZE = 32
N = 64
SPAN = 128
ROWS = 4
LEN = 512
SEND = 32
N_CTX = 4


def shuffled_rows(key, count, length):
    subkeys = jax.random.split(key, count)

    def shuffle_one(subkey):
        return jax.random.permutation(subkey, jnp.arange(length, dtype=jnp.int32))
    return jax.vmap(shuffle_one)(subkeys)


def draw_pack_place(key, part):
    key = jax.random.fold_in(key, 11)
    target_sets = shuffled_rows(jax.random.fold_in(key, 1), ROWS * N_CTX, SPAN).reshape(ROWS, N_CTX, SPAN)
    target_sets = target_sets + (jnp.arange(N_CTX, dtype=jnp.int32) * SPAN)[None, :, None]
    target_sets = target_sets.reshape(ROWS, N_CTX, N_CTX, SEND).transpose(0, 2, 1, 3).reshape(ROWS, N_CTX, SPAN)
    mixing = shuffled_rows(jax.random.fold_in(key, 2), ROWS * N_CTX, SPAN).reshape(ROWS, N_CTX, SPAN)
    placed = jnp.take_along_axis(target_sets, mixing, axis=2)
    return placed.reshape(ROWS, LEN).astype(jnp.int32)


def draw_doc_starts(key, part):
    key = jax.random.fold_in(key, 23)
    picks = jax.random.randint(key, (ROWS, LEN), 0, 2 * SPAN)
    leading = jnp.arange(LEN, dtype=jnp.int32)[None, :] == 0
    return jnp.where(leading | (picks == 0), 1, 0).astype(jnp.int32)


def shard_levels(stream_key, dims, shards, low, top_value):
    level = 1.0
    for axis_at, parts in shards:
        draws = jax.random.uniform(jax.random.fold_in(jax.random.fold_in(stream_key, 6), axis_at), (parts,), jnp.float32, low / len(shards), top_value / len(shards))
        level = level * jnp.repeat(jnp.exp(draws), dims[axis_at] // parts).reshape((-1,) + (1,) * (len(dims) - 1 - axis_at))
    return level


def scatter_about(key, dims, scale, most, cuts=(), kind=jnp.bfloat16):
    entries = scale * jax.random.normal(key, dims, jnp.float32)
    if cuts:
        entries = entries * shard_levels(key, dims, cuts, -0.22, 0.18)
    return jnp.clip(entries, -most, most).astype(kind)


def setup_inputs(seed: int = 0, part: int = 0) -> dict:
    keys = jax.random.split(jax.random.key(seed), 10)
    own_keys = jax.random.split(jax.random.fold_in(keys[9], part), 10)
    return {
        "layer_input": scatter_about(own_keys[0], (ROWS, LEN, D), 1.0, 6.0, ((0, 4), (1, 4))),
        "head_input": scatter_about(own_keys[1], (ROWS, LEN, H * P_SIZE), 1.0, 6.0, ((0, 4), (1, 4))),
        "input_map": scatter_about(own_keys[2], (ROWS, LEN, N), 0.3, 2.0, ((0, 4), (1, 4))),
        "output_map": scatter_about(own_keys[3], (ROWS, LEN, N), 0.04, 0.25, ((0, 4), (1, 4))),
        "step_weight": scatter_about(keys[4], (D, H), D ** -0.5, 0.09375, ((0, 16),)),
        "decay_log": jnp.clip(jax.random.uniform(keys[5], (H,), jnp.float32, -9.0, -3.0), -9.0, -3.0),
        "pack_place": draw_pack_place(jax.random.fold_in(jax.random.fold_in(keys[9], part), 71), part),
        "doc_starts": draw_doc_starts(jax.random.fold_in(jax.random.fold_in(keys[9], part), 71), part),
        "out_grad": scatter_about(own_keys[8], (ROWS, LEN, H * P_SIZE), 0.25, 1.5, ((0, 4), (1, 4))),
    }


HIGHEST_PRECISION = lax.Precision.HIGHEST

def contract(form, *operands):
    return jnp.einsum(form, *operands, precision=HIGHEST_PRECISION)

def row_forward(raw_step, head_vals, in_map, out_map, decay_log, start_row):
    decay_rate = jnp.exp(decay_log)
    step_size = jax.nn.softplus(raw_step)
    log_decay = -step_size * decay_rate[None, :]
    block_count = head_vals.shape[0] // SPAN

    def block_split(array):
        return array.reshape((block_count, SPAN) + array.shape[1:])
    positions = jnp.arange(SPAN, dtype=jnp.int32)
    causal = positions[:, None] >= positions[None, :]

    def advance(carry_state, block_data):
        x_block, step_block, decay_block, b_block, c_block, start_block = block_data
        cumul = jnp.cumsum(decay_block, axis=0)
        segment = jnp.cumsum(start_block)
        joined = (segment[:, None] == segment[None, :]) & causal
        spread = cumul.T[:, :, None] - cumul.T[:, None, :]
        kernel = jnp.where(joined[None], jnp.exp(jnp.where(joined[None], spread, 0.0)), 0.0)
        gram = contract('in,jn->ij', c_block, b_block)
        scaled = x_block * step_block[:, :, None]
        intra = contract('hij,jhp->ihp', kernel * gram[None], scaled)
        alive = (segment == 0).astype(jnp.float32)
        enter = jnp.exp(cumul) * alive[:, None]
        inter = contract('ih,hpn,in->ihp', enter, carry_state, c_block)
        tail_mask = (segment == segment[-1]).astype(jnp.float32)
        leave = jnp.exp(cumul[-1:] - cumul) * tail_mask[:, None]
        end_state = contract('jh,jhp,jn->hpn', leave, scaled, b_block)
        decay_total = jnp.exp(cumul[-1]) * alive[-1]
        next_state = decay_total[:, None, None] * carry_state + end_state
        return (next_state, intra + inter)
    initial = jnp.zeros((head_vals.shape[1], head_vals.shape[2], in_map.shape[1]), jnp.float32)
    _, outputs = lax.scan(advance, initial, (block_split(head_vals), block_split(step_size), block_split(log_decay), block_split(in_map), block_split(out_map), block_split(start_row)))
    return outputs.reshape(head_vals.shape)

def reference(layer_input, head_input, input_map, output_map, step_weight, decay_log, pack_place, doc_starts, out_grad):
    row_count, length, model_dim = layer_input.shape
    head_count = step_weight.shape[1]
    head_dim = head_input.shape[2] // head_count
    row_index = jnp.arange(row_count, dtype=jnp.int32)[:, None]

    def packed(array):
        return jnp.zeros_like(array).at[row_index, pack_place].set(array)
    u_packed = packed(layer_input)
    x_packed = packed(head_input)
    b_packed = packed(input_map)
    c_packed = packed(output_map)
    raw_bf = jnp.dot(u_packed.reshape(-1, model_dim), step_weight, preferred_element_type=jnp.float32).astype(jnp.bfloat16)
    raw_bf = lax.optimization_barrier(raw_bf)
    raw_step = raw_bf.astype(jnp.float32).reshape(row_count, length, head_count)
    x_heads = x_packed.astype(jnp.float32).reshape(row_count, length, head_count, head_dim)
    b_full = b_packed.astype(jnp.float32)
    c_full = c_packed.astype(jnp.float32)
    cotangent = out_grad.astype(jnp.float32).reshape(row_count, length, head_count, head_dim)

    def one_row(row_data):
        raw_row, x_row, b_row, c_row, start_row, grad_row = row_data

        def objective(raw_arg, x_arg, b_arg, c_arg):
            return jnp.sum(row_forward(raw_arg, x_arg, b_arg, c_arg, decay_log, start_row) * grad_row)
        return jax.grad(objective, argnums=(0, 1, 2, 3))(raw_row, x_row, b_row, c_row)
    grad_raw, grad_x, grad_b, grad_c = lax.map(one_row, (raw_step, x_heads, b_full, c_full, doc_starts, cotangent))
    weight_grad = lax.dot_general(u_packed.reshape(-1, model_dim).astype(jnp.float32), grad_raw.reshape(-1, head_count), (((0,), (0,)), ((), ())), precision=HIGHEST_PRECISION)
    head_grad = grad_x.reshape(row_count, length, head_count * head_dim).astype(jnp.bfloat16)
    return (head_grad, grad_b, grad_c, weight_grad)
```

```python
import functools

import jax
import jax.numpy as jnp
from jax import lax
from jax.experimental import pallas as pl
from jax.experimental.pallas import tpu as pltpu
from jax.sharding import PartitionSpec as P

HIGHEST_PRECISION = lax.Precision.HIGHEST


def carried_in(array, axis, combine, identity, reverse):
    size, mine = (lax.axis_size(axis), lax.axis_index(axis))
    everything = jax.tree.map(lambda part: lax.all_gather(part, axis), array)
    start = jax.tree.map(
        lambda part, zero: jnp.broadcast_to(jnp.asarray(zero, part.dtype), part.shape),
        array,
        identity,
    )

    def turn(k, before):
        at = size - 1 - k if reverse else k
        reached = at > mine if reverse else at < mine
        new = combine(before, jax.tree.map(lambda part: part[at], everything))
        return jax.tree.map(lambda a, b: jnp.where(reached, a, b), new, before)

    return lax.fori_loop(0, size, turn, start)


def contract(form, *operands):
    return jnp.einsum(form, *operands, precision=HIGHEST_PRECISION)


def chain_link(earlier, later):
    return (earlier[0] * later[0], later[1] + later[0][:, :, None, None] * earlier[1])


def route_slots(pack_place, block_len):
    shard_index = lax.axis_index("ctx")
    local_place = lax.dynamic_slice_in_dim(pack_place, shard_index * block_len, block_len, 1)
    sender_order = jnp.argsort(local_place, axis=1)
    targets = shard_index * block_len + jnp.arange(block_len, dtype=jnp.int32)
    all_positions = jnp.arange(pack_place.shape[1], dtype=jnp.int32)
    matches = pack_place[:, None, :] == targets[None, :, None]
    anchor = jnp.sum(jnp.where(matches, all_positions[None, None, :], 0), axis=2) // block_len
    positions = jnp.arange(block_len, dtype=jnp.int32)
    before = positions[None, :] < positions[:, None]
    same_anchor = (anchor[:, :, None] == anchor[:, None, :]) & before[None]
    rank_within = jnp.sum(same_anchor.astype(jnp.int32), axis=2)
    return (sender_order, anchor * (block_len // lax.axis_size("ctx")) + rank_within)


def on_device(
    layer_input,
    head_input,
    input_map,
    output_map,
    step_weight,
    decay_log,
    pack_place,
    doc_starts,
    out_grad,
):
    shard_count = lax.axis_size("ctx")
    rows_dev, block_len, inner_width = head_input.shape
    head_count = decay_log.shape[0]
    head_dim = inner_width // head_count
    model_dim = layer_input.shape[2]
    send_rows = block_len // shard_count
    sender_order, slot_index = route_slots(pack_place, block_len)

    def for_sending(array):
        ordered = jnp.take_along_axis(array, sender_order[:, :, None], axis=1)
        return ordered.reshape(rows_dev, shard_count, send_rows, array.shape[2])

    def packed_order(received):
        flat_rows = received.reshape(rows_dev, block_len, received.shape[3])
        return jnp.take_along_axis(flat_rows, slot_index[:, :, None], axis=1)

    flat_rows = layer_input.reshape(rows_dev * block_len, model_dim)
    columns = flat_rows
    summed = jnp.dot(
        columns,
        lax.all_gather(step_weight, ("ctx", "dp"), axis=0, tiled=True),
        preferred_element_type=jnp.float32,
    )
    raw_local = lax.optimization_barrier(summed.astype(jnp.bfloat16)).reshape(
        rows_dev, block_len, head_count
    )
    received = (
        lax.all_to_all(for_sending(head_input), "ctx", split_axis=1, concat_axis=1, tiled=True),
        lax.all_to_all(for_sending(input_map), "ctx", split_axis=1, concat_axis=1, tiled=True),
        lax.all_to_all(for_sending(output_map), "ctx", split_axis=1, concat_axis=1, tiled=True),
        lax.all_to_all(for_sending(raw_local), "ctx", split_axis=1, concat_axis=1, tiled=True),
    )
    x_packed = packed_order(received[0])
    b_packed = packed_order(received[1])
    c_packed = packed_order(received[2])
    raw_packed = packed_order(received[3])
    decay_rate = jnp.exp(decay_log)
    raw_step = raw_packed.astype(jnp.float32)
    step_size = jax.nn.softplus(raw_step)
    log_decay = -step_size * decay_rate[None, None, :]
    cumul = jnp.cumsum(log_decay, axis=1)
    segment = jnp.cumsum(doc_starts, axis=1)
    alive = (segment == 0).astype(jnp.float32)
    positions = jnp.arange(block_len, dtype=jnp.int32)
    causal = positions[:, None] >= positions[None, :]
    joined = ((segment[:, :, None] == segment[:, None, :]) & causal[None])[:, None]
    cumul_heads = jnp.transpose(cumul, (0, 2, 1))
    spread = cumul_heads[:, :, :, None] - cumul_heads[:, :, None, :]
    kernel = jnp.where(joined, jnp.exp(jnp.where(joined, spread, 0.0)), 0.0)
    x_heads = x_packed.astype(jnp.float32).reshape(rows_dev, block_len, head_count, head_dim)
    b_full = b_packed.astype(jnp.float32)
    c_full = c_packed.astype(jnp.float32)
    scaled = x_heads * step_size[:, :, :, None]
    gram = contract("rin,rjn->rij", c_full, b_full)
    weighted = kernel * gram[:, None]
    enter = jnp.exp(cumul) * alive[:, :, None]
    tail_mask = (segment == segment[:, -1:]).astype(jnp.float32)
    leave = jnp.exp(cumul[:, -1:, :] - cumul) * tail_mask[:, :, None]
    end_state = contract("rjh,rjhp,rjn->rhpn", leave, scaled, b_full)
    decay_total = jnp.exp(cumul[:, -1, :]) * alive[:, -1:]
    identity = (jnp.ones_like(decay_total), jnp.zeros_like(end_state))
    state_in = carried_in((decay_total, end_state), "ctx", chain_link, identity, False)[1]
    cotangent = out_grad.astype(jnp.float32).reshape(rows_dev, block_len, head_count, head_dim)
    local_back = contract("rih,rihp,rin->rhpn", enter, cotangent, c_full)
    state_grad = carried_in((decay_total, local_back), "ctx", chain_link, identity, True)[1]
    grad_scaled = contract("rhij,rihp->rjhp", weighted, cotangent) + contract(
        "rjh,rhpn,rjn->rjhp", leave, state_grad, b_full
    )
    grad_weighted = contract("rihp,rjhp->rhij", cotangent, scaled)
    grad_gram = jnp.sum(kernel * grad_weighted, axis=1)
    product = weighted * grad_weighted
    grad_cumul = jnp.transpose(jnp.sum(product, axis=3) - jnp.sum(product, axis=2), (0, 2, 1))
    readout = contract("rhpn,rin->rihp", state_in, c_full)
    grad_cumul = grad_cumul + enter * jnp.sum(cotangent * readout, axis=3)
    flow = contract("rjhp,rhpn,rjn->rjh", scaled, state_grad, b_full) * leave
    grad_cumul = grad_cumul - flow
    last_extra = jnp.sum(flow, axis=1) + decay_total * jnp.sum(state_grad * state_in, axis=(2, 3))
    grad_cumul = grad_cumul.at[:, -1, :].add(last_extra)
    grad_log = jnp.flip(jnp.cumsum(jnp.flip(grad_cumul, 1), axis=1), 1)
    grad_step = jnp.sum(x_heads * grad_scaled, axis=3) - decay_rate[None, None, :] * grad_log
    grad_raw = grad_step * jax.nn.sigmoid(raw_step)
    head_grad = (
        (grad_scaled * step_size[:, :, :, None])
        .reshape(rows_dev, block_len, inner_width)
        .astype(jnp.bfloat16)
    )
    grad_c = contract("rij,rjn->rin", grad_gram, b_full) + contract(
        "rih,rihp,rhpn->rin", enter, cotangent, state_in
    )
    grad_b = contract("rij,rin->rjn", grad_gram, c_full) + contract(
        "rjh,rjhp,rhpn->rjn", leave, scaled, state_grad
    )
    inverse_slot = jnp.argsort(slot_index, axis=1)
    arranged = jnp.take_along_axis(grad_raw, inverse_slot[:, :, None], axis=1).reshape(
        rows_dev, shard_count, send_rows, head_count
    )
    returned = lax.all_to_all(arranged, "ctx", split_axis=1, concat_axis=1, tiled=True).reshape(
        rows_dev, block_len, head_count
    )
    inverse_order = jnp.argsort(sender_order, axis=1)
    grad_rows = jnp.take_along_axis(returned, inverse_order[:, :, None], axis=1)
    source_rows = layer_input.reshape(rows_dev * block_len, model_dim)
    grad_flat = grad_rows.reshape(rows_dev * block_len, head_count)
    columns = source_rows.astype(jnp.float32)
    weight_grad = lax.psum_scatter(
        lax.dot_general(columns, grad_flat, (((0,), (0,)), ((), ())), precision=HIGHEST_PRECISION),
        ("ctx", "dp"),
        scatter_dimension=0,
        tiled=True,
    )
    return (head_grad, grad_b, grad_c, weight_grad)


def mm(a, b):
    return jnp.dot(a, b, preferred_element_type=jnp.float32)


def nt(a, b, precision=None):
    return lax.dot_general(
        a, b, (((1,), (1,)), ((), ())), precision=precision, preferred_element_type=jnp.float32
    )


def one_hot(mask, kind=jnp.bfloat16):
    return jnp.where(mask, 1.0, 0.0).astype(kind)


def iotas(rows, columns):
    return (
        lax.broadcasted_iota(jnp.int32, (rows, columns), 0),
        lax.broadcasted_iota(jnp.int32, (rows, columns), 1),
    )


def eye(size, kind=jnp.bfloat16):
    row, column = iotas(size, size)
    return one_hot(row == column, kind)


def two_parts(array):
    high = array.astype(jnp.bfloat16)
    return high, (array - high.astype(jnp.float32)).astype(jnp.bfloat16)


def remote(src, dst, send_sem, recv_sem, **where):
    return pltpu.make_async_remote_copy(
        src_ref=src,
        dst_ref=dst,
        send_sem=send_sem,
        recv_sem=recv_sem,
        device_id=where,
        device_id_type=pl.DeviceIdType.MESH,
    )


def layer_kernel(
    dims,
    u_ref, x_ref, b_ref, c_ref, w_ref, log_ref, place_ref, start_ref, g_ref,
    dx_ref, db_ref, dc_ref, dw_ref,
    wall, us, uall, xs, xr, bcs, bcr, raws, rawr, xp,
    step_wide, enter_wide, leave_wide, y_acc, gs_acc, eg, lx,
    end_own, back_own, end_all, f_out, f_in, g_out, g_in,
    cum_col, cum_row, step_row, gram_grad, gsl, gall, ps, pr,
    wz_s, wz_r, wd_s, wd_r, u_s, u_r, x_s, x_r, bc_s, bc_r, raw_s, raw_r,
    f_s, f_r, b_s, b_r, g_s, g_r, p_s, p_r,
):
    n, m, length, heads, head_dim, state, chunks = dims
    f32, bf = jnp.float32, jnp.bfloat16
    me, mine = lax.axis_index("ctx"), lax.axis_index("dp")
    rows = length // n
    block = w_ref.shape[0]
    width = heads * head_dim
    wide = width // chunks
    per = 128 // head_dim

    def z_peer(k):
        return lax.rem(me + k, n)

    def d_peer(k):
        return lax.rem(mine + k, m)

    def piece(k):
        return pl.ds(pl.multiple_of(k * rows, rows), rows)

    barrier = pltpu.get_barrier_semaphore()
    for kz in range(n):
        for kd in range(m):
            if kz or kd:
                pl.semaphore_signal(
                    barrier, inc=1, device_id={"ctx": z_peer(kz), "dp": d_peer(kd)},
                    device_id_type=pl.DeviceIdType.MESH,
                )

    wall[mine, me] = nt(eye(heads), w_ref[...]).astype(bf)
    row, column = iotas(length, length)
    row_f = row.astype(f32)
    before = one_hot(row < column)
    lower = one_hot(row >= column)

    def prefix(flags):
        return mm(jnp.broadcast_to(flags, (8, length)).astype(bf), before)[0:1]

    own_place = jnp.zeros((1, length), jnp.int32)
    for k in range(n):
        own_place = jnp.where(me == k, place_ref[:, k * length : (k + 1) * length], own_place)
    slot = jnp.zeros((1, length), f32)
    for k in range(n):
        flags = one_hot((own_place >= k * length) & (own_place < (k + 1) * length), f32)
        slot = slot + flags * (k * rows + prefix(flags))
    p_send = one_hot(slot == row_f)
    pl.semaphore_wait(barrier, n * m - 1)

    w_z = []
    for k in range(1, n):
        copy = remote(
            wall.at[mine, me], wall.at[mine, me], wz_s.at[k], wz_r.at[k], ctx=z_peer(k), dp=mine
        )
        copy.start()
        w_z.append(copy)

    xs[...] = mm(p_send, x_ref[...]).astype(bf)
    bcs[0] = mm(p_send, b_ref[...]).astype(bf)
    bcs[1] = mm(p_send, c_ref[...]).astype(bf)
    x_copies, bc_copies = [], []
    for k in range(1, n):
        to = z_peer(k)
        copy = remote(
            bcs.at[:, piece(to)], bcr.at[:, piece(me)], bc_s.at[k], bc_r.at[k], ctx=to, dp=mine
        )
        copy.start()
        bc_copies.append(copy)
    for k in range(1, n):
        to = z_peer(k)
        copy = remote(xs.at[piece(to)], xr.at[piece(me)], x_s.at[k], x_r.at[k], ctx=to, dp=mine)
        copy.start()
        x_copies.append(copy)
    bcr[:, piece(me)] = bcs[:, piece(me)]
    xr[piece(me)] = xs[piece(me)]

    for copy in w_z:
        copy.wait_recv()
    w_d = []
    for k in range(1, m):
        copy = remote(
            wall.at[mine], wall.at[mine], wd_s.at[k], wd_r.at[k], ctx=me, dp=d_peer(k)
        )
        copy.start()
        w_d.append(copy)

    for d in range(m):
        for z in range(n):
            at = (z * m + d) * block
            us[d, :, z * block : (z + 1) * block] = mm(
                p_send, u_ref[:, at : at + block]
            ).astype(bf)
    u_copies = []
    for k in range(1, m):
        to = d_peer(k)
        copy = remote(us.at[to], uall.at[mine], u_s.at[k], u_r.at[k], ctx=me, dp=to)
        copy.start()
        u_copies.append(copy)
    uall[mine] = us[mine]

    p_recv = jnp.zeros((length, length), f32)
    p_back = jnp.zeros((length, length), f32)
    for k in range(n):
        place = place_ref[:, k * length : (k + 1) * length] - me * length
        here = (place >= 0) & (place < length)
        rank = jnp.where(here, k * rows + prefix(one_hot(here, f32)), -1.0)
        lands = one_hot(place == row)
        comes = one_hot(rank == row_f)
        p_recv = p_recv + nt(lands, comes)
        p_back = p_back + nt(comes, lands)
    p_recv, p_back = p_recv.astype(bf), p_back.astype(bf)

    starts = jnp.broadcast_to(start_ref[...].astype(f32), (8, length)).astype(bf)
    seg_col = nt(lower, starts)[:, 0:1]
    seg_row = nt(starts, lower)[0:1]
    seg_last = seg_row[:, length - 1 : length]
    joined = (seg_col == seg_row) & (row >= column)
    joined_t = (seg_col == seg_row) & (row <= column)
    alive = one_hot(seg_col == 0.0, f32)
    tail = one_hot(seg_col == seg_last, f32)
    alive_last = one_hot(seg_last == 0.0, f32)

    raw = jnp.zeros((length, heads), f32)
    for k in range(m):
        if k:
            w_d[k - 1].wait_recv()
        part = lax.rem(mine + m - k, m)
        for z in range(n):
            raw = raw + nt(us[part, :, z * block : (z + 1) * block], wall[part, z])
    raws[...] = raw.astype(bf)
    raw_copies = []
    for k in range(1, n):
        to = z_peer(k)
        copy = remote(
            raws.at[piece(to)], rawr.at[piece(me)], raw_s.at[k], raw_r.at[k], ctx=to, dp=mine
        )
        copy.start()
        raw_copies.append(copy)
    rawr[piece(me)] = raws[piece(me)]

    for copy in bc_copies:
        copy.wait_recv()
    b_pack = mm(p_recv, bcr[0]).astype(bf)
    c_pack = mm(p_recv, bcr[1]).astype(bf)
    b_turn = nt(eye(state), b_pack).astype(bf)
    c_turn = nt(eye(state), c_pack).astype(bf)
    gram = nt(c_pack, b_pack)
    gram_t = nt(b_pack, c_pack)
    for copy in x_copies:
        copy.wait_recv()
    xp[...] = mm(p_recv, xr[...]).astype(bf)
    head_row, head_column = iotas(heads, width)
    spread = one_hot(
        (head_column >= head_row * head_dim) & (head_column < (head_row + 1) * head_dim)
    )

    def expand(array):
        high, low = two_parts(array)
        return mm(high, spread) + mm(low, spread)

    for copy in raw_copies:
        copy.wait_recv()
    raw_step = mm(p_recv, rawr[...])
    rate = jnp.exp(log_ref[...])
    step = jnp.maximum(raw_step, 0.0) + jnp.log1p(jnp.exp(-jnp.abs(raw_step)))
    log_decay = -step * rate
    cumul = jnp.dot(
        lower.astype(f32), log_decay, precision=HIGHEST_PRECISION, preferred_element_type=f32
    )
    total = cumul[length - 1 : length]
    decay_total = jnp.exp(total) * alive_last
    decay_wide = expand(jnp.broadcast_to(decay_total, (8, heads)))[0:1]
    step_wide[...] = expand(step)
    enter_wide[...] = expand(jnp.exp(cumul) * alive)
    leave_wide[...] = expand(jnp.exp(total - cumul) * tail)
    eg[...] = (enter_wide[...] * g_ref[...].astype(f32)).astype(bf)
    lx[...] = (leave_wide[...] * step_wide[...] * xp[...].astype(f32)).astype(bf)

    def lanes(c):
        return slice(c * wide, (c + 1) * wide)

    f_copies = [
        remote(f_out.at[c], f_in.at[c], f_s.at[c], f_r.at[c], ctx=lax.rem(me + 1, n), dp=mine)
        for c in range(chunks)
    ]
    b_copies = [
        remote(g_out.at[c], g_in.at[c], b_s.at[c], b_r.at[c], ctx=lax.rem(me + n - 1, n), dp=mine)
        for c in range(chunks)
    ]
    for c in range(chunks):
        end_own[c] = mm(b_turn, lx[:, lanes(c)])

        @pl.when(me == 0)
        def _():
            f_in[c] = jnp.zeros((state, wide), f_in.dtype)
            f_out[c] = end_own[c].astype(f_out.dtype)
            f_copies[c].start()

        back_own[c] = mm(c_turn, eg[:, lanes(c)])

        @pl.when(me == n - 1)
        def _():
            g_in[c] = jnp.zeros((state, wide), g_in.dtype)
            g_out[c] = back_own[c].astype(g_out.dtype)
            b_copies[c].start()

    eye_f = eye(heads, f32)
    cum_row[...] = nt(eye_f, cumul, HIGHEST_PRECISION)
    step_row[...] = nt(eye_f, step, HIGHEST_PRECISION)
    for k in range(heads // per):
        cum_col[k, :, 0:per] = cumul[:, k * per : (k + 1) * per]
    gram_grad[...] = jnp.zeros_like(gram_grad)
    lane_head = lax.broadcasted_iota(jnp.int32, (length, 128), 1)

    def only(array, q):
        return jnp.where(
            (lane_head >= q * head_dim) & (lane_head < (q + 1) * head_dim), array, 0.0
        ).astype(bf)

    def intra(at, _):
        here = pl.ds(pl.multiple_of(at * 128, 128), 128)
        g4 = g_ref[:, here].astype(f32)
        x4 = xp[:, here].astype(f32)
        s4 = x4 * step_wide[:, here]
        stack = lambda array: jnp.concatenate([only(array, q) for q in range(per)], axis=0)
        inner = nt(g4.astype(bf), stack(x4))
        weights, turned = [], []
        columns = cum_col[at]
        grown = gram_grad[...]
        for q in range(per):
            across = cum_row[pl.ds(at * per + q, 1), :]
            down = columns[:, q : q + 1]
            apart = down - across
            kernel = jnp.where(joined, jnp.exp(apart), 0.0)
            kernel_t = jnp.where(joined_t, jnp.exp(-apart), 0.0)
            scale = step_row[pl.ds(at * per + q, 1), :]
            grown = grown + kernel * (inner[:, q * length : (q + 1) * length] * scale)
            weights.append((kernel * gram).astype(bf))
            turned.append((kernel_t * gram_t).astype(bf))
        gram_grad[...] = grown
        y_acc[:, here] = mm(jnp.concatenate(weights, axis=1), stack(s4))
        gs_acc[:, here] = mm(jnp.concatenate(turned, axis=1), stack(g4))
        return 0

    grad_c = jnp.zeros((length, state), f32)
    grad_b = jnp.zeros((length, state), f32)
    out_sum = jnp.zeros((length, heads), f32)
    in_sum = jnp.zeros((length, heads), f32)
    last_extra = jnp.zeros((8, heads), f32)
    groups = heads // per // chunks
    for c in range(chunks):
        lax.fori_loop(c * groups, (c + 1) * groups, intra, 0)

        @pl.when(me > 0)
        def _():
            f_copies[c].wait_recv()

        end_all[c] = decay_wide[:, lanes(c)] * f_in[c].astype(f32) + end_own[c]

        @pl.when((me > 0) & (me < n - 1))
        def _():
            f_out[c] = end_all[c].astype(f_out.dtype)
            f_copies[c].start()

        @pl.when(me < n - 1)
        def _():
            b_copies[c].wait_recv()

        @pl.when((me > 0) & (me < n - 1))
        def _():
            g_out[c] = (
                decay_wide[:, lanes(c)] * g_in[c].astype(f32) + back_own[c]
            ).astype(g_out.dtype)
            b_copies[c].start()

        state_in, state_grad = f_in[c].astype(bf), g_in[c].astype(bf)
        y = y_acc[:, lanes(c)] + enter_wide[:, lanes(c)] * mm(c_pack, state_in)
        grad_scaled = gs_acc[:, lanes(c)] + leave_wide[:, lanes(c)] * mm(b_pack, state_grad)
        dx_ref[:, lanes(c)] = (grad_scaled * step_wide[:, lanes(c)]).astype(bf)
        members = spread[:, lanes(c)]

        def head_sum(array):
            high, low = two_parts(array)
            return nt(high, members) + nt(low, members)

        out_sum = out_sum + head_sum(g_ref[:, lanes(c)].astype(f32) * y)
        in_sum = in_sum + head_sum(xp[:, lanes(c)].astype(f32) * grad_scaled)
        met = jnp.sum(g_in[c].astype(f32) * end_all[c], axis=0, keepdims=True)
        last_extra = last_extra + head_sum(jnp.broadcast_to(met, (8, wide)))
        grad_c = grad_c + nt(eg[:, lanes(c)], state_in)
        grad_b = grad_b + nt(lx[:, lanes(c)], state_grad)

    grad_cumul = out_sum - step * in_sum
    grad_log = (
        jnp.dot(
            one_hot(row <= column, f32),
            grad_cumul,
            precision=HIGHEST_PRECISION,
            preferred_element_type=f32,
        )
        + last_extra[0:1]
    )
    grad_raw = (in_sum - rate * grad_log) / (1.0 + jnp.exp(-raw_step))
    gsl[...] = mm(p_back, grad_raw.astype(bf)).astype(bf)
    gall[mine, piece(me)] = gsl[piece(me)]
    g_copies = []
    for kz in range(n):
        for kd in range(m):
            if kz or kd:
                to = z_peer(kz)
                copy = remote(
                    gsl.at[piece(to)], gall.at[mine, piece(me)], g_s.at[kz, kd], g_r.at[kz, kd],
                    ctx=to, dp=d_peer(kd),
                )
                copy.start()
                g_copies.append(copy)

    gram_b = gram_grad[...].astype(bf)
    dc_ref[...] = grad_c + mm(gram_b, b_pack)
    db_ref[...] = grad_b + mm(nt(eye(length), gram_b).astype(bf), c_pack)

    for copy in u_copies:
        copy.wait_recv()
    for copy in g_copies:
        copy.wait_recv()
    eye_b = eye(heads)
    turned_grads = [nt(eye_b, gall[d]).astype(bf) for d in range(m)]

    def weight_part(z):
        part = jnp.zeros((heads, block), f32)
        for d in range(m):
            part = part + mm(
                turned_grads[d],
                uall[d, :, pl.ds(pl.multiple_of(z * block, block), block)],
            )
        return part

    p_copies = []
    for k in range(1, n):
        to = z_peer(k)
        ps[k] = weight_part(to).astype(ps.dtype)
        copy = remote(ps.at[k], pr.at[k], p_s.at[k], p_r.at[k], ctx=to, dp=mine)
        copy.start()
        p_copies.append(copy)
    summed = weight_part(me)
    for k, copy in enumerate(p_copies):
        copy.wait_recv()
        summed = summed + pr[k + 1].astype(f32)
    dw_ref[...] = nt(eye(block, f32), summed, HIGHEST_PRECISION)

    for copy in w_z + w_d + u_copies + x_copies + bc_copies + raw_copies + g_copies + p_copies:
        copy.wait_send()
    for c in range(chunks):

        @pl.when(me < n - 1)
        def _():
            f_copies[c].wait_send()

        @pl.when(me > 0)
        def _():
            b_copies[c].wait_send()


def fits(n, m, rows_dev, length, heads, head_dim, state, block):
    return (
        rows_dev == 1
        and length == 128
        and (length // n) % 16 == 0
        and 128 % head_dim == 0
        and heads * head_dim % 512 == 0
        and heads % 8 == 0
        and block % 128 == 0
    )


def on_device_fused(
    layer_input,
    head_input,
    input_map,
    output_map,
    step_weight,
    decay_log,
    pack_place,
    doc_starts,
    out_grad,
):
    n, m = lax.axis_size("ctx"), lax.axis_size("dp")
    _, length, width = head_input.shape
    heads, state, model = decay_log.shape[0], input_map.shape[2], layer_input.shape[2]
    block = step_weight.shape[0]
    chunks = 4
    wide = width // chunks
    per = 128 // (width // heads)
    f32, bf = jnp.float32, jnp.bfloat16
    dims = (n, m, length, heads, width // heads, state, chunks)
    vmem, dma = pltpu.VMEM, pltpu.SemaphoreType.DMA
    whole = pl.BlockSpec(memory_space=pltpu.VMEM)
    scratch = [
        vmem((m, n, heads, block), bf),
        vmem((m, length, n * block), bf),
        vmem((m, length, n * block), bf),
        vmem((length, width), bf),
        vmem((length, width), bf),
        vmem((2, length, state), bf),
        vmem((2, length, state), bf),
        vmem((length, heads), bf),
        vmem((length, heads), bf),
        vmem((length, width), bf),
        vmem((length, width), f32),
        vmem((length, width), f32),
        vmem((length, width), f32),
        vmem((length, width), f32),
        vmem((length, width), f32),
        vmem((length, width), bf),
        vmem((length, width), bf),
        vmem((chunks, state, wide), f32),
        vmem((chunks, state, wide), f32),
        vmem((chunks, state, wide), f32),
        vmem((chunks, state, wide), bf),
        vmem((chunks, state, wide), bf),
        vmem((chunks, state, wide), bf),
        vmem((chunks, state, wide), bf),
        vmem((heads // per, length, 128), f32),
        vmem((heads, length), f32),
        vmem((heads, length), f32),
        vmem((length, length), f32),
        vmem((length, heads), bf),
        vmem((m, length, heads), bf),
        vmem((n, heads, block), bf),
        vmem((n, heads, block), bf),
        dma((n,)), dma((n,)), dma((m,)), dma((m,)), dma((m,)), dma((m,)),
        dma((n,)), dma((n,)), dma((n,)), dma((n,)), dma((n,)), dma((n,)),
        dma((chunks,)), dma((chunks,)), dma((chunks,)), dma((chunks,)),
        dma((n, m)), dma((n, m)), dma((n,)), dma((n,)),
    ]
    head_grad, grad_b, grad_c, weight_grad = pl.pallas_call(
        functools.partial(layer_kernel, dims),
        out_shape=(
            jax.ShapeDtypeStruct((length, width), bf),
            jax.ShapeDtypeStruct((length, state), f32),
            jax.ShapeDtypeStruct((length, state), f32),
            jax.ShapeDtypeStruct((block, heads), f32),
        ),
        in_specs=[whole] * 9,
        out_specs=(whole,) * 4,
        scratch_shapes=scratch,
        compiler_params=pltpu.CompilerParams(
            collective_id=0, has_side_effects=True, vmem_limit_bytes=48 * 1024 * 1024
        ),
    )(
        layer_input[0],
        head_input[0],
        input_map[0],
        output_map[0],
        step_weight,
        decay_log[None],
        pack_place,
        doc_starts,
        out_grad[0],
    )
    return head_grad[None], grad_b[None], grad_c[None], weight_grad


def solution(mesh):
    placed = (
        P(("groups", "dp"), "ctx", None),
        P(("groups", "dp"), "ctx", None),
        P(("groups", "dp"), "ctx", None),
        P(("groups", "dp"), "ctx", None),
        P(("ctx", "dp"), None),
        P(),
        P(("groups", "dp"), None),
        P(("groups", "dp"), "ctx"),
        P(("groups", "dp"), "ctx", None),
    )

    def chosen(*arrays):
        n, m = mesh.shape["ctx"], mesh.shape["dp"]
        rows_dev, length, width = arrays[1].shape
        heads = arrays[5].shape[0]
        sizes = (rows_dev, length, heads, width // heads, arrays[2].shape[2], arrays[4].shape[0])
        return (on_device_fused if fits(n, m, *sizes) else on_device)(*arrays)

    return jax.shard_map(
        chosen,
        mesh=mesh,
        in_specs=placed,
        out_specs=(
            P(("groups", "dp"), "ctx", None),
            P(("groups", "dp"), "ctx", None),
            P(("groups", "dp"), "ctx", None),
            P(("groups", "ctx", "dp"), None),
        ),
        check_vma=False,
    )
```

```python
import functools

import jax
import jax.numpy as jnp
from jax import lax
from jax.experimental import pallas as pl
from jax.experimental.pallas import tpu as pltpu
from jax.sharding import PartitionSpec as P

HIGHEST_PRECISION = lax.Precision.HIGHEST


def carried_in(array, axis, combine, identity, reverse):
    size, mine = (lax.axis_size(axis), lax.axis_index(axis))
    everything = jax.tree.map(lambda part: lax.all_gather(part, axis), array)
    start = jax.tree.map(
        lambda part, zero: jnp.broadcast_to(jnp.asarray(zero, part.dtype), part.shape),
        array,
        identity,
    )

    def turn(k, before):
        at = size - 1 - k if reverse else k
        reached = at > mine if reverse else at < mine
        new = combine(before, jax.tree.map(lambda part: part[at], everything))
        return jax.tree.map(lambda a, b: jnp.where(reached, a, b), new, before)

    return lax.fori_loop(0, size, turn, start)


def contract(form, *operands):
    return jnp.einsum(form, *operands, precision=HIGHEST_PRECISION)


def chain_link(earlier, later):
    return (earlier[0] * later[0], later[1] + later[0][:, :, None, None] * earlier[1])


def route_slots(pack_place, block_len):
    shard_index = lax.axis_index("ctx")
    local_place = lax.dynamic_slice_in_dim(pack_place, shard_index * block_len, block_len, 1)
    sender_order = jnp.argsort(local_place, axis=1)
    targets = shard_index * block_len + jnp.arange(block_len, dtype=jnp.int32)
    all_positions = jnp.arange(pack_place.shape[1], dtype=jnp.int32)
    matches = pack_place[:, None, :] == targets[None, :, None]
    anchor = jnp.sum(jnp.where(matches, all_positions[None, None, :], 0), axis=2) // block_len
    positions = jnp.arange(block_len, dtype=jnp.int32)
    before = positions[None, :] < positions[:, None]
    same_anchor = (anchor[:, :, None] == anchor[:, None, :]) & before[None]
    rank_within = jnp.sum(same_anchor.astype(jnp.int32), axis=2)
    return (sender_order, anchor * (block_len // lax.axis_size("ctx")) + rank_within)


def on_device(
    layer_input,
    head_input,
    input_map,
    output_map,
    step_weight,
    decay_log,
    pack_place,
    doc_starts,
    out_grad,
):
    shard_count = lax.axis_size("ctx")
    rows_dev, block_len, inner_width = head_input.shape
    head_count = decay_log.shape[0]
    head_dim = inner_width // head_count
    model_dim = layer_input.shape[2]
    send_rows = block_len // shard_count
    sender_order, slot_index = route_slots(pack_place, block_len)

    def for_sending(array):
        ordered = jnp.take_along_axis(array, sender_order[:, :, None], axis=1)
        return ordered.reshape(rows_dev, shard_count, send_rows, array.shape[2])

    def packed_order(received):
        flat_rows = received.reshape(rows_dev, block_len, received.shape[3])
        return jnp.take_along_axis(flat_rows, slot_index[:, :, None], axis=1)

    flat_rows = layer_input.reshape(rows_dev * block_len, model_dim)
    columns = flat_rows
    summed = jnp.dot(
        columns,
        lax.all_gather(step_weight, ("ctx", "dp"), axis=0, tiled=True),
        preferred_element_type=jnp.float32,
    )
    raw_local = lax.optimization_barrier(summed.astype(jnp.bfloat16)).reshape(
        rows_dev, block_len, head_count
    )
    received = (
        lax.all_to_all(for_sending(head_input), "ctx", split_axis=1, concat_axis=1, tiled=True),
        lax.all_to_all(for_sending(input_map), "ctx", split_axis=1, concat_axis=1, tiled=True),
        lax.all_to_all(for_sending(output_map), "ctx", split_axis=1, concat_axis=1, tiled=True),
        lax.all_to_all(for_sending(raw_local), "ctx", split_axis=1, concat_axis=1, tiled=True),
    )
    x_packed = packed_order(received[0])
    b_packed = packed_order(received[1])
    c_packed = packed_order(received[2])
    raw_packed = packed_order(received[3])
    decay_rate = jnp.exp(decay_log)
    raw_step = raw_packed.astype(jnp.float32)
    step_size = jax.nn.softplus(raw_step)
    log_decay = -step_size * decay_rate[None, None, :]
    cumul = jnp.cumsum(log_decay, axis=1)
    segment = jnp.cumsum(doc_starts, axis=1)
    alive = (segment == 0).astype(jnp.float32)
    positions = jnp.arange(block_len, dtype=jnp.int32)
    causal = positions[:, None] >= positions[None, :]
    joined = ((segment[:, :, None] == segment[:, None, :]) & causal[None])[:, None]
    cumul_heads = jnp.transpose(cumul, (0, 2, 1))
    spread = cumul_heads[:, :, :, None] - cumul_heads[:, :, None, :]
    kernel = jnp.where(joined, jnp.exp(jnp.where(joined, spread, 0.0)), 0.0)
    x_heads = x_packed.astype(jnp.float32).reshape(rows_dev, block_len, head_count, head_dim)
    b_full = b_packed.astype(jnp.float32)
    c_full = c_packed.astype(jnp.float32)
    scaled = x_heads * step_size[:, :, :, None]
    gram = contract("rin,rjn->rij", c_full, b_full)
    weighted = kernel * gram[:, None]
    enter = jnp.exp(cumul) * alive[:, :, None]
    tail_mask = (segment == segment[:, -1:]).astype(jnp.float32)
    leave = jnp.exp(cumul[:, -1:, :] - cumul) * tail_mask[:, :, None]
    end_state = contract("rjh,rjhp,rjn->rhpn", leave, scaled, b_full)
    decay_total = jnp.exp(cumul[:, -1, :]) * alive[:, -1:]
    identity = (jnp.ones_like(decay_total), jnp.zeros_like(end_state))
    state_in = carried_in((decay_total, end_state), "ctx", chain_link, identity, False)[1]
    cotangent = out_grad.astype(jnp.float32).reshape(rows_dev, block_len, head_count, head_dim)
    local_back = contract("rih,rihp,rin->rhpn", enter, cotangent, c_full)
    state_grad = carried_in((decay_total, local_back), "ctx", chain_link, identity, True)[1]
    grad_scaled = contract("rhij,rihp->rjhp", weighted, cotangent) + contract(
        "rjh,rhpn,rjn->rjhp", leave, state_grad, b_full
    )
    grad_weighted = contract("rihp,rjhp->rhij", cotangent, scaled)
    grad_gram = jnp.sum(kernel * grad_weighted, axis=1)
    product = weighted * grad_weighted
    grad_cumul = jnp.transpose(jnp.sum(product, axis=3) - jnp.sum(product, axis=2), (0, 2, 1))
    readout = contract("rhpn,rin->rihp", state_in, c_full)
    grad_cumul = grad_cumul + enter * jnp.sum(cotangent * readout, axis=3)
    flow = contract("rjhp,rhpn,rjn->rjh", scaled, state_grad, b_full) * leave
    grad_cumul = grad_cumul - flow
    last_extra = jnp.sum(flow, axis=1) + decay_total * jnp.sum(state_grad * state_in, axis=(2, 3))
    grad_cumul = grad_cumul.at[:, -1, :].add(last_extra)
    grad_log = jnp.flip(jnp.cumsum(jnp.flip(grad_cumul, 1), axis=1), 1)
    grad_step = jnp.sum(x_heads * grad_scaled, axis=3) - decay_rate[None, None, :] * grad_log
    grad_raw = grad_step * jax.nn.sigmoid(raw_step)
    head_grad = (
        (grad_scaled * step_size[:, :, :, None])
        .reshape(rows_dev, block_len, inner_width)
        .astype(jnp.bfloat16)
    )
    grad_c = contract("rij,rjn->rin", grad_gram, b_full) + contract(
        "rih,rihp,rhpn->rin", enter, cotangent, state_in
    )
    grad_b = contract("rij,rin->rjn", grad_gram, c_full) + contract(
        "rjh,rjhp,rhpn->rjn", leave, scaled, state_grad
    )
    inverse_slot = jnp.argsort(slot_index, axis=1)
    arranged = jnp.take_along_axis(grad_raw, inverse_slot[:, :, None], axis=1).reshape(
        rows_dev, shard_count, send_rows, head_count
    )
    returned = lax.all_to_all(arranged, "ctx", split_axis=1, concat_axis=1, tiled=True).reshape(
        rows_dev, block_len, head_count
    )
    inverse_order = jnp.argsort(sender_order, axis=1)
    grad_rows = jnp.take_along_axis(returned, inverse_order[:, :, None], axis=1)
    source_rows = layer_input.reshape(rows_dev * block_len, model_dim)
    grad_flat = grad_rows.reshape(rows_dev * block_len, head_count)
    columns = source_rows.astype(jnp.float32)
    weight_grad = lax.psum_scatter(
        lax.dot_general(columns, grad_flat, (((0,), (0,)), ((), ())), precision=HIGHEST_PRECISION),
        ("ctx", "dp"),
        scatter_dimension=0,
        tiled=True,
    )
    return (head_grad, grad_b, grad_c, weight_grad)


def mm(a, b):
    return jnp.dot(a, b, preferred_element_type=jnp.float32)


def nt(a, b, precision=None):
    return lax.dot_general(
        a, b, (((1,), (1,)), ((), ())), precision=precision, preferred_element_type=jnp.float32
    )


def one_hot(mask, kind=jnp.bfloat16):
    return jnp.where(mask, 1.0, 0.0).astype(kind)


def iotas(rows, columns):
    return (
        lax.broadcasted_iota(jnp.int32, (rows, columns), 0),
        lax.broadcasted_iota(jnp.int32, (rows, columns), 1),
    )


def eye(size, kind=jnp.bfloat16):
    row, column = iotas(size, size)
    return one_hot(row == column, kind)


def two_parts(array):
    high = array.astype(jnp.bfloat16)
    return high, (array - high.astype(jnp.float32)).astype(jnp.bfloat16)


def remote(src, dst, send_sem, recv_sem, **where):
    return pltpu.make_async_remote_copy(
        src_ref=src,
        dst_ref=dst,
        send_sem=send_sem,
        recv_sem=recv_sem,
        device_id=where,
        device_id_type=pl.DeviceIdType.MESH,
    )


def layer_kernel(
    dims,
    u_hbm, x_hbm, b_hbm, c_hbm, w_hbm, log_hbm, place_hbm, start_hbm, g_hbm,
    dx_ref, db_ref, dc_ref, dw_ref,
    u_ref, x_ref, bc_ref, log_ref, place_ref, start_ref, g_ref,
    wall, us, uall, xs, xr, bcs, bcr, raws, rawr, xp,
    step_wide, enter_wide, leave_wide, y_acc, gs_acc, eg, lx,
    end_own, back_own, f_out, f_in, g_out, g_in,
    cum_col, cum_row, step_row, gram_grad, gsl, gall, ps, pr,
    wz_s, wz_r, wd_s, wd_r, u_s, u_r, x_s, x_r, bc_s, bc_r, raw_s, raw_r,
    f_s, f_r, b_s, b_r, g_s, g_r, p_s, p_r, in_s,
):
    n, m, length, heads, head_dim, state, chunks = dims
    f32, bf = jnp.float32, jnp.bfloat16
    me, mine = lax.axis_index("ctx"), lax.axis_index("dp")
    rows = length // n
    block = w_hbm.shape[1]
    width = heads * head_dim
    wide = width // chunks
    per = 128 // head_dim

    def z_peer(k):
        return lax.rem(me + k, n)

    def d_peer(k):
        return lax.rem(mine + k, m)

    def piece(k):
        return pl.ds(pl.multiple_of(k * rows, rows), rows)

    barrier = pltpu.get_barrier_semaphore()
    for kz in range(n):
        for kd in range(m):
            if kz or kd:
                pl.semaphore_signal(
                    barrier, inc=1, device_id={"ctx": z_peer(kz), "dp": d_peer(kd)},
                    device_id_type=pl.DeviceIdType.MESH,
                )

    loads = [
        pltpu.make_async_copy(src, dst, in_s.at[k])
        for k, (src, dst) in enumerate(
            (
                (place_hbm, place_ref),
                (w_hbm, wall.at[mine, me]),
                (x_hbm, x_ref),
                (b_hbm, bc_ref.at[0:state]),
                (c_hbm, bc_ref.at[state : 2 * state]),
                (u_hbm, u_ref),
                (start_hbm, start_ref),
                (log_hbm, log_ref),
                (g_hbm, g_ref),
            )
        )
    ]
    for load in loads:
        load.start()
    row, column = iotas(length, length)
    row_f = row.astype(f32)
    before = one_hot(row < column)
    lower = one_hot(row >= column)

    def prefix(flags):
        return mm(jnp.broadcast_to(flags, (8, length)).astype(bf), before)[0:1]

    loads[0].wait()
    own_place = jnp.zeros((1, length), jnp.int32)
    for k in range(n):
        own_place = jnp.where(me == k, place_ref[:, k * length : (k + 1) * length], own_place)
    slot = jnp.zeros((1, length), f32)
    for k in range(n):
        flags = one_hot((own_place >= k * length) & (own_place < (k + 1) * length), f32)
        slot = slot + flags * (k * rows + prefix(flags))
    p_send = one_hot(slot == row_f)
    loads[1].wait()
    pl.semaphore_wait(barrier, n * m - 1)

    w_z = []
    for k in range(1, n):
        copy = remote(
            wall.at[mine, me], wall.at[mine, me], wz_s.at[k], wz_r.at[k], ctx=z_peer(k), dp=mine
        )
        copy.start()
        w_z.append(copy)

    for load in loads[2:6]:
        load.wait()
    xs[...] = mm(p_send, x_ref[...]).astype(bf)
    bcs[...] = nt(p_send, bc_ref[...]).astype(bf)
    for copy in w_z:
        copy.wait_recv()
    w_d = []
    for k in range(1, m):
        copy = remote(
            wall.at[mine], wall.at[mine], wd_s.at[k], wd_r.at[k], ctx=me, dp=d_peer(k)
        )
        copy.start()
        w_d.append(copy)
    x_copies, bc_copies = [], []
    for k in range(1, n):
        to = z_peer(k)
        copy = remote(
            bcs.at[piece(to)], bcr.at[piece(me)], bc_s.at[k], bc_r.at[k], ctx=to, dp=mine
        )
        copy.start()
        bc_copies.append(copy)
    for k in range(1, n):
        to = z_peer(k)
        copy = remote(xs.at[piece(to)], xr.at[piece(me)], x_s.at[k], x_r.at[k], ctx=to, dp=mine)
        copy.start()
        x_copies.append(copy)
    bcr[piece(me)] = bcs[piece(me)]
    xr[piece(me)] = xs[piece(me)]

    for d in range(m):
        for z in range(n):
            at = (z * m + d) * block
            us[d, :, z * block : (z + 1) * block] = mm(
                p_send, u_ref[:, at : at + block]
            ).astype(bf)
    uall[mine] = us[mine]

    p_recv = jnp.zeros((length, length), f32)
    p_back = jnp.zeros((length, length), f32)
    for k in range(n):
        place = place_ref[:, k * length : (k + 1) * length] - me * length
        here = (place >= 0) & (place < length)
        rank = jnp.where(here, k * rows + prefix(one_hot(here, f32)), -1.0)
        lands = one_hot(place == row)
        comes = one_hot(rank == row_f)
        p_recv = p_recv + nt(lands, comes)
        p_back = p_back + nt(comes, lands)
    p_recv, p_back = p_recv.astype(bf), p_back.astype(bf)

    for load in loads[6:]:
        load.wait()
    starts = jnp.broadcast_to(start_ref[...].astype(f32), (8, length)).astype(bf)
    seg_col = nt(lower, starts)[:, 0:1]
    seg_row = nt(starts, lower)[0:1]
    seg_last = seg_row[:, length - 1 : length]
    joined = (seg_col == seg_row) & (row >= column)
    joined_t = (seg_col == seg_row) & (row <= column)
    alive = one_hot(seg_col == 0.0, f32)
    tail = one_hot(seg_col == seg_last, f32)
    alive_last = one_hot(seg_last == 0.0, f32)

    raw = jnp.zeros((length, heads), f32)
    for k in range(m):
        if k:
            w_d[k - 1].wait_recv()
        part = lax.rem(mine + m - k, m)
        for z in range(n):
            raw = raw + nt(us[part, :, z * block : (z + 1) * block], wall[part, z])
    raws[...] = raw.astype(bf)
    raw_copies = []
    for k in range(1, n):
        to = z_peer(k)
        copy = remote(
            raws.at[piece(to)], rawr.at[piece(me)], raw_s.at[k], raw_r.at[k], ctx=to, dp=mine
        )
        copy.start()
        raw_copies.append(copy)
    rawr[piece(me)] = raws[piece(me)]
    u_copies = []
    for k in range(1, m):
        to = d_peer(k)
        copy = remote(us.at[to], uall.at[mine], u_s.at[k], u_r.at[k], ctx=me, dp=to)
        copy.start()
        u_copies.append(copy)

    for copy in bc_copies:
        copy.wait_recv()
    both = mm(p_recv, bcr[...]).astype(bf)
    b_pack, c_pack = both[:, :state], both[:, state:]
    both_turned = nt(eye(2 * state), both).astype(bf)
    b_turn, c_turn = both_turned[:state], both_turned[state:]
    gram = nt(c_pack, b_pack)
    gram_t = nt(b_pack, c_pack)
    for copy in x_copies:
        copy.wait_recv()
    xp[...] = mm(p_recv, xr[...]).astype(bf)
    head_row, head_column = iotas(heads, width)
    spread = one_hot(
        (head_column >= head_row * head_dim) & (head_column < (head_row + 1) * head_dim)
    )

    def expand(array):
        high, low = two_parts(array)
        return mm(high, spread) + mm(low, spread)

    for copy in raw_copies:
        copy.wait_recv()
    raw_step = mm(p_recv, rawr[...])
    rate = jnp.exp(log_ref[...])
    step = jnp.maximum(raw_step, 0.0) + jnp.log1p(jnp.exp(-jnp.abs(raw_step)))
    log_decay = -step * rate
    cumul = jnp.dot(
        lower.astype(f32), log_decay, precision=HIGHEST_PRECISION, preferred_element_type=f32
    )
    total = cumul[length - 1 : length]
    decay_total = jnp.exp(total) * alive_last
    decay_wide = expand(jnp.broadcast_to(decay_total, (8, heads)))[0:1]
    step_wide[...] = expand(step)
    enter_wide[...] = expand(jnp.exp(cumul) * alive)
    leave_wide[...] = expand(jnp.exp(total - cumul) * tail)
    eg[...] = (enter_wide[...] * g_ref[...].astype(f32)).astype(bf)
    lx[...] = (leave_wide[...] * step_wide[...] * xp[...].astype(f32)).astype(bf)

    def lanes(c):
        return slice(c * wide, (c + 1) * wide)

    f_copies = [
        remote(f_out.at[c], f_in.at[c], f_s.at[c], f_r.at[c], ctx=lax.rem(me + 1, n), dp=mine)
        for c in range(chunks)
    ]
    b_copies = [
        remote(g_out.at[c], g_in.at[c], b_s.at[c], b_r.at[c], ctx=lax.rem(me + n - 1, n), dp=mine)
        for c in range(chunks)
    ]
    for c in range(chunks):
        end_own[c] = mm(b_turn, lx[:, lanes(c)])

        @pl.when(me == 0)
        def _():
            f_in[c] = jnp.zeros((state, wide), f_in.dtype)
            f_out[c] = end_own[c].astype(f_out.dtype)
            f_copies[c].start()

        back_own[c] = mm(c_turn, eg[:, lanes(c)])

        @pl.when(me == n - 1)
        def _():
            g_in[c] = jnp.zeros((state, wide), g_in.dtype)
            g_out[c] = back_own[c].astype(g_out.dtype)
            b_copies[c].start()

    eye_f = eye(heads, f32)
    cum_row[...] = nt(eye_f, cumul, HIGHEST_PRECISION)
    step_row[...] = nt(eye_f, step, HIGHEST_PRECISION)
    for k in range(heads // per):
        cum_col[k, :, 0:per] = cumul[:, k * per : (k + 1) * per]
    gram_grad[...] = jnp.zeros_like(gram_grad)
    lane_head = lax.broadcasted_iota(jnp.int32, (length, 128), 1)

    def only(array, q):
        return jnp.where(
            (lane_head >= q * head_dim) & (lane_head < (q + 1) * head_dim), array, 0.0
        ).astype(bf)

    def intra(at, _):
        here = pl.ds(pl.multiple_of(at * 128, 128), 128)
        g4 = g_ref[:, here].astype(f32)
        x4 = xp[:, here].astype(f32)
        s4 = x4 * step_wide[:, here]
        stack = lambda array: jnp.concatenate([only(array, q) for q in range(per)], axis=0)
        inner = nt(g4.astype(bf), stack(x4))
        weights, turned = [], []
        columns = cum_col[at]
        grown = gram_grad[...]
        for q in range(per):
            across = cum_row[pl.ds(at * per + q, 1), :]
            down = columns[:, q : q + 1]
            apart = down - across
            kernel = jnp.where(joined, jnp.exp(apart), 0.0)
            kernel_t = jnp.where(joined_t, jnp.exp(-apart), 0.0)
            scale = step_row[pl.ds(at * per + q, 1), :]
            grown = grown + kernel * (inner[:, q * length : (q + 1) * length] * scale)
            weights.append((kernel * gram).astype(bf))
            turned.append((kernel_t * gram_t).astype(bf))
        gram_grad[...] = grown
        y_acc[:, here] = mm(jnp.concatenate(weights, axis=1), stack(s4))
        gs_acc[:, here] = mm(jnp.concatenate(turned, axis=1), stack(g4))
        return 0

    grad_c = jnp.zeros((state, length), f32)
    grad_b = jnp.zeros((state, length), f32)
    out_sum = jnp.zeros((length, heads), f32)
    in_sum = jnp.zeros((length, heads), f32)
    last_extra = jnp.zeros((8, heads), f32)
    groups = heads // per // chunks

    def relay_forward(c):
        @pl.when(me > 0)
        def _():
            f_copies[c].wait_recv()

        @pl.when((me > 0) & (me < n - 1))
        def _():
            f_out[c] = (
                decay_wide[:, lanes(c)] * f_in[c].astype(f32) + end_own[c]
            ).astype(f_out.dtype)
            f_copies[c].start()

    def relay_back(c):
        @pl.when(me < n - 1)
        def _():
            b_copies[c].wait_recv()

        @pl.when((me > 0) & (me < n - 1))
        def _():
            g_out[c] = (
                decay_wide[:, lanes(c)] * g_in[c].astype(f32) + back_own[c]
            ).astype(g_out.dtype)
            b_copies[c].start()

    for c in range(chunks):
        lax.fori_loop(c * groups, (c + 1) * groups, intra, 0)

        @pl.when(me < n // 2)
        def _():
            relay_forward(c)

        @pl.when(me >= n // 2)
        def _():
            relay_back(c)

    for c in range(chunks):

        @pl.when(me < n // 2)
        def _():
            relay_back(c)

        @pl.when(me >= n // 2)
        def _():
            relay_forward(c)

        end_all = decay_wide[:, lanes(c)] * f_in[c].astype(f32) + end_own[c]
        state_in, state_grad = f_in[c].astype(bf), g_in[c].astype(bf)
        y = y_acc[:, lanes(c)] + enter_wide[:, lanes(c)] * mm(c_pack, state_in)
        grad_scaled = gs_acc[:, lanes(c)] + leave_wide[:, lanes(c)] * mm(b_pack, state_grad)
        dx_ref[:, lanes(c)] = (grad_scaled * step_wide[:, lanes(c)]).astype(bf)
        members = spread[:, lanes(c)]

        def head_sum(array):
            high, low = two_parts(array)
            return nt(high, members) + nt(low, members)

        out_sum = out_sum + head_sum(g_ref[:, lanes(c)].astype(f32) * y)
        in_sum = in_sum + head_sum(xp[:, lanes(c)].astype(f32) * grad_scaled)
        met = jnp.sum(g_in[c].astype(f32) * end_all, axis=0, keepdims=True)
        last_extra = last_extra + head_sum(jnp.broadcast_to(met, (8, wide)))
        grad_c = grad_c + nt(state_in, eg[:, lanes(c)])
        grad_b = grad_b + nt(state_grad, lx[:, lanes(c)])

    grad_cumul = out_sum - step * in_sum
    grad_log = (
        jnp.dot(
            one_hot(row <= column, f32),
            grad_cumul,
            precision=HIGHEST_PRECISION,
            preferred_element_type=f32,
        )
        + last_extra[0:1]
    )
    grad_raw = (in_sum - rate * grad_log) / (1.0 + jnp.exp(-raw_step))
    gsl[...] = mm(p_back, jnp.concatenate(two_parts(grad_raw), axis=1)).astype(bf)
    gall[mine, piece(me)] = gsl[piece(me)]
    g_copies = []
    for kz in range(n):
        for kd in range(m):
            if kz or kd:
                to = z_peer(kz)
                copy = remote(
                    gsl.at[piece(to)], gall.at[mine, piece(me)], g_s.at[kz, kd], g_r.at[kz, kd],
                    ctx=to, dp=d_peer(kd),
                )
                copy.start()
                g_copies.append(copy)

    gram_b = gram_grad[...].astype(bf)
    dc_ref[...] = grad_c + nt(b_turn, gram_b)
    db_ref[...] = grad_b + mm(c_turn, gram_b)

    for copy in u_copies:
        copy.wait_recv()
    for copy in g_copies:
        copy.wait_recv()
    eye_b = eye(2 * heads)
    turned_grads = [nt(eye_b, gall[d]).astype(bf) for d in range(m)]

    def weight_part(z):
        part = jnp.zeros((2 * heads, block), f32)
        for d in range(m):
            part = part + mm(
                turned_grads[d],
                uall[d, :, pl.ds(pl.multiple_of(z * block, block), block)],
            )
        return part[:heads] + part[heads:]

    p_copies = []
    for k in range(1, n):
        to = z_peer(k)
        ps[k] = weight_part(to).astype(ps.dtype)
        copy = remote(ps.at[k], pr.at[k], p_s.at[k], p_r.at[k], ctx=to, dp=mine)
        copy.start()
        p_copies.append(copy)
    summed = weight_part(me)
    for k, copy in enumerate(p_copies):
        copy.wait_recv()
        summed = summed + pr[k + 1].astype(f32)
    dw_ref[...] = summed

    for copy in w_z + w_d + u_copies + x_copies + bc_copies + raw_copies + g_copies + p_copies:
        copy.wait_send()
    for c in range(chunks):

        @pl.when(me < n - 1)
        def _():
            f_copies[c].wait_send()

        @pl.when(me > 0)
        def _():
            b_copies[c].wait_send()


def hand_over(*refs):
    half = len(refs) // 2
    for source, target in zip(refs[:half], refs[half:]):
        target[...] = source[...]


def fits(n, m, rows_dev, length, heads, head_dim, state, block):
    return (
        rows_dev == 1
        and length == 128
        and (length // n) % 16 == 0
        and 128 % head_dim == 0
        and heads * head_dim % 512 == 0
        and heads % 8 == 0
        and block % 128 == 0
    )


def on_device_fused(
    layer_input,
    head_input,
    input_map,
    output_map,
    step_weight,
    decay_log,
    pack_place,
    doc_starts,
    out_grad,
):
    n, m = lax.axis_size("ctx"), lax.axis_size("dp")
    _, length, width = head_input.shape
    heads, state, model = decay_log.shape[0], input_map.shape[2], layer_input.shape[2]
    block = step_weight.shape[0]
    chunks = 4
    wide = width // chunks
    per = 128 // (width // heads)
    f32, bf = jnp.float32, jnp.bfloat16
    dims = (n, m, length, heads, width // heads, state, chunks)
    vmem, dma = pltpu.VMEM, pltpu.SemaphoreType.DMA
    whole = pl.BlockSpec(memory_space=pltpu.VMEM)
    scratch = [
        vmem((length, n * m * block), bf),
        vmem((length, width), bf),
        vmem((2 * state, length), bf),
        vmem((1, heads), f32),
        vmem((1, n * length), jnp.int32),
        vmem((1, length), jnp.int32),
        vmem((length, width), bf),
        vmem((m, n, heads, block), bf),
        vmem((m, length, n * block), bf),
        vmem((m, length, n * block), bf),
        vmem((length, width), bf),
        vmem((length, width), bf),
        vmem((length, 2 * state), bf),
        vmem((length, 2 * state), bf),
        vmem((length, heads), bf),
        vmem((length, heads), bf),
        vmem((length, width), bf),
        vmem((length, width), f32),
        vmem((length, width), f32),
        vmem((length, width), f32),
        vmem((length, width), f32),
        vmem((length, width), f32),
        vmem((length, width), bf),
        vmem((length, width), bf),
        vmem((chunks, state, wide), f32),
        vmem((chunks, state, wide), f32),
        vmem((chunks, state, wide), bf),
        vmem((chunks, state, wide), bf),
        vmem((chunks, state, wide), bf),
        vmem((chunks, state, wide), bf),
        vmem((heads // per, length, 128), f32),
        vmem((heads, length), f32),
        vmem((heads, length), f32),
        vmem((length, length), f32),
        vmem((length, 2 * heads), bf),
        vmem((m, length, 2 * heads), bf),
        vmem((n, heads, block), bf),
        vmem((n, heads, block), bf),
        dma((n,)), dma((n,)), dma((m,)), dma((m,)), dma((m,)), dma((m,)),
        dma((n,)), dma((n,)), dma((n,)), dma((n,)), dma((n,)), dma((n,)),
        dma((chunks,)), dma((chunks,)), dma((chunks,)), dma((chunks,)),
        dma((n, m)), dma((n, m)), dma((n,)), dma((n,)), dma((9,)),
    ]
    results = (
        jax.ShapeDtypeStruct((length, width), bf),
        jax.ShapeDtypeStruct((state, length), f32),
        jax.ShapeDtypeStruct((state, length), f32),
        jax.ShapeDtypeStruct((heads, block), f32),
    )
    grads = pl.pallas_call(
        functools.partial(layer_kernel, dims),
        out_shape=results,
        in_specs=[pl.BlockSpec(memory_space=pltpu.HBM)] * 9,
        out_specs=(whole,) * 4,
        scratch_shapes=scratch,
        compiler_params=pltpu.CompilerParams(
            collective_id=0, has_side_effects=True, vmem_limit_bytes=56 * 1024 * 1024
        ),
    )(
        layer_input[0],
        head_input[0],
        input_map[0].T,
        output_map[0].T,
        step_weight.T,
        decay_log[None],
        pack_place,
        doc_starts,
        out_grad[0],
    )
    head_grad, grad_b, grad_c, weight_grad = pl.pallas_call(
        hand_over, out_shape=results, in_specs=[whole] * 4, out_specs=(whole,) * 4
    )(*grads)
    return head_grad[None], grad_b.T[None], grad_c.T[None], weight_grad.T


def solution(mesh):
    placed = (
        P(("groups", "dp"), "ctx", None),
        P(("groups", "dp"), "ctx", None),
        P(("groups", "dp"), "ctx", None),
        P(("groups", "dp"), "ctx", None),
        P(("ctx", "dp"), None),
        P(),
        P(("groups", "dp"), None),
        P(("groups", "dp"), "ctx"),
        P(("groups", "dp"), "ctx", None),
    )

    def chosen(*arrays):
        n, m = mesh.shape["ctx"], mesh.shape["dp"]
        rows_dev, length, width = arrays[1].shape
        heads = arrays[5].shape[0]
        sizes = (rows_dev, length, heads, width // heads, arrays[2].shape[2], arrays[4].shape[0])
        return (on_device_fused if fits(n, m, *sizes) else on_device)(*arrays)

    return jax.shard_map(
        chosen,
        mesh=mesh,
        in_specs=placed,
        out_specs=(
            P(("groups", "dp"), "ctx", None),
            P(("groups", "dp"), "ctx", None),
            P(("groups", "dp"), "ctx", None),
            P(("groups", "ctx", "dp"), None),
        ),
        check_vma=False,
    )
```

```python
import functools

import jax
import jax.numpy as jnp
from jax import lax
from jax.experimental import pallas as pl
from jax.experimental.pallas import tpu as pltpu
from jax.sharding import PartitionSpec as P

HIGHEST_PRECISION = lax.Precision.HIGHEST


def carried_in(array, axis, combine, identity, reverse):
    size, mine = (lax.axis_size(axis), lax.axis_index(axis))
    everything = jax.tree.map(lambda part: lax.all_gather(part, axis), array)
    start = jax.tree.map(
        lambda part, zero: jnp.broadcast_to(jnp.asarray(zero, part.dtype), part.shape),
        array,
        identity,
    )

    def turn(k, before):
        at = size - 1 - k if reverse else k
        reached = at > mine if reverse else at < mine
        new = combine(before, jax.tree.map(lambda part: part[at], everything))
        return jax.tree.map(lambda a, b: jnp.where(reached, a, b), new, before)

    return lax.fori_loop(0, size, turn, start)


def contract(form, *operands):
    return jnp.einsum(form, *operands, precision=HIGHEST_PRECISION)


def chain_link(earlier, later):
    return (earlier[0] * later[0], later[1] + later[0][:, :, None, None] * earlier[1])


def route_slots(pack_place, block_len):
    shard_index = lax.axis_index("ctx")
    local_place = lax.dynamic_slice_in_dim(pack_place, shard_index * block_len, block_len, 1)
    sender_order = jnp.argsort(local_place, axis=1)
    targets = shard_index * block_len + jnp.arange(block_len, dtype=jnp.int32)
    all_positions = jnp.arange(pack_place.shape[1], dtype=jnp.int32)
    matches = pack_place[:, None, :] == targets[None, :, None]
    anchor = jnp.sum(jnp.where(matches, all_positions[None, None, :], 0), axis=2) // block_len
    positions = jnp.arange(block_len, dtype=jnp.int32)
    before = positions[None, :] < positions[:, None]
    same_anchor = (anchor[:, :, None] == anchor[:, None, :]) & before[None]
    rank_within = jnp.sum(same_anchor.astype(jnp.int32), axis=2)
    return (sender_order, anchor * (block_len // lax.axis_size("ctx")) + rank_within)


def on_device(
    layer_input,
    head_input,
    input_map,
    output_map,
    step_weight,
    decay_log,
    pack_place,
    doc_starts,
    out_grad,
):
    shard_count = lax.axis_size("ctx")
    rows_dev, block_len, inner_width = head_input.shape
    head_count = decay_log.shape[0]
    head_dim = inner_width // head_count
    model_dim = layer_input.shape[2]
    send_rows = block_len // shard_count
    sender_order, slot_index = route_slots(pack_place, block_len)

    def for_sending(array):
        ordered = jnp.take_along_axis(array, sender_order[:, :, None], axis=1)
        return ordered.reshape(rows_dev, shard_count, send_rows, array.shape[2])

    def packed_order(received):
        flat_rows = received.reshape(rows_dev, block_len, received.shape[3])
        return jnp.take_along_axis(flat_rows, slot_index[:, :, None], axis=1)

    flat_rows = layer_input.reshape(rows_dev * block_len, model_dim)
    columns = flat_rows
    summed = jnp.dot(
        columns,
        lax.all_gather(step_weight, ("ctx", "dp"), axis=0, tiled=True),
        preferred_element_type=jnp.float32,
    )
    raw_local = lax.optimization_barrier(summed.astype(jnp.bfloat16)).reshape(
        rows_dev, block_len, head_count
    )
    received = (
        lax.all_to_all(for_sending(head_input), "ctx", split_axis=1, concat_axis=1, tiled=True),
        lax.all_to_all(for_sending(input_map), "ctx", split_axis=1, concat_axis=1, tiled=True),
        lax.all_to_all(for_sending(output_map), "ctx", split_axis=1, concat_axis=1, tiled=True),
        lax.all_to_all(for_sending(raw_local), "ctx", split_axis=1, concat_axis=1, tiled=True),
    )
    x_packed = packed_order(received[0])
    b_packed = packed_order(received[1])
    c_packed = packed_order(received[2])
    raw_packed = packed_order(received[3])
    decay_rate = jnp.exp(decay_log)
    raw_step = raw_packed.astype(jnp.float32)
    step_size = jax.nn.softplus(raw_step)
    log_decay = -step_size * decay_rate[None, None, :]
    cumul = jnp.cumsum(log_decay, axis=1)
    segment = jnp.cumsum(doc_starts, axis=1)
    alive = (segment == 0).astype(jnp.float32)
    positions = jnp.arange(block_len, dtype=jnp.int32)
    causal = positions[:, None] >= positions[None, :]
    joined = ((segment[:, :, None] == segment[:, None, :]) & causal[None])[:, None]
    cumul_heads = jnp.transpose(cumul, (0, 2, 1))
    spread = cumul_heads[:, :, :, None] - cumul_heads[:, :, None, :]
    kernel = jnp.where(joined, jnp.exp(jnp.where(joined, spread, 0.0)), 0.0)
    x_heads = x_packed.astype(jnp.float32).reshape(rows_dev, block_len, head_count, head_dim)
    b_full = b_packed.astype(jnp.float32)
    c_full = c_packed.astype(jnp.float32)
    scaled = x_heads * step_size[:, :, :, None]
    gram = contract("rin,rjn->rij", c_full, b_full)
    weighted = kernel * gram[:, None]
    enter = jnp.exp(cumul) * alive[:, :, None]
    tail_mask = (segment == segment[:, -1:]).astype(jnp.float32)
    leave = jnp.exp(cumul[:, -1:, :] - cumul) * tail_mask[:, :, None]
    end_state = contract("rjh,rjhp,rjn->rhpn", leave, scaled, b_full)
    decay_total = jnp.exp(cumul[:, -1, :]) * alive[:, -1:]
    identity = (jnp.ones_like(decay_total), jnp.zeros_like(end_state))
    state_in = carried_in((decay_total, end_state), "ctx", chain_link, identity, False)[1]
    cotangent = out_grad.astype(jnp.float32).reshape(rows_dev, block_len, head_count, head_dim)
    local_back = contract("rih,rihp,rin->rhpn", enter, cotangent, c_full)
    state_grad = carried_in((decay_total, local_back), "ctx", chain_link, identity, True)[1]
    grad_scaled = contract("rhij,rihp->rjhp", weighted, cotangent) + contract(
        "rjh,rhpn,rjn->rjhp", leave, state_grad, b_full
    )
    grad_weighted = contract("rihp,rjhp->rhij", cotangent, scaled)
    grad_gram = jnp.sum(kernel * grad_weighted, axis=1)
    product = weighted * grad_weighted
    grad_cumul = jnp.transpose(jnp.sum(product, axis=3) - jnp.sum(product, axis=2), (0, 2, 1))
    readout = contract("rhpn,rin->rihp", state_in, c_full)
    grad_cumul = grad_cumul + enter * jnp.sum(cotangent * readout, axis=3)
    flow = contract("rjhp,rhpn,rjn->rjh", scaled, state_grad, b_full) * leave
    grad_cumul = grad_cumul - flow
    last_extra = jnp.sum(flow, axis=1) + decay_total * jnp.sum(state_grad * state_in, axis=(2, 3))
    grad_cumul = grad_cumul.at[:, -1, :].add(last_extra)
    grad_log = jnp.flip(jnp.cumsum(jnp.flip(grad_cumul, 1), axis=1), 1)
    grad_step = jnp.sum(x_heads * grad_scaled, axis=3) - decay_rate[None, None, :] * grad_log
    grad_raw = grad_step * jax.nn.sigmoid(raw_step)
    head_grad = (
        (grad_scaled * step_size[:, :, :, None])
        .reshape(rows_dev, block_len, inner_width)
        .astype(jnp.bfloat16)
    )
    grad_c = contract("rij,rjn->rin", grad_gram, b_full) + contract(
        "rih,rihp,rhpn->rin", enter, cotangent, state_in
    )
    grad_b = contract("rij,rin->rjn", grad_gram, c_full) + contract(
        "rjh,rjhp,rhpn->rjn", leave, scaled, state_grad
    )
    inverse_slot = jnp.argsort(slot_index, axis=1)
    arranged = jnp.take_along_axis(grad_raw, inverse_slot[:, :, None], axis=1).reshape(
        rows_dev, shard_count, send_rows, head_count
    )
    returned = lax.all_to_all(arranged, "ctx", split_axis=1, concat_axis=1, tiled=True).reshape(
        rows_dev, block_len, head_count
    )
    inverse_order = jnp.argsort(sender_order, axis=1)
    grad_rows = jnp.take_along_axis(returned, inverse_order[:, :, None], axis=1)
    source_rows = layer_input.reshape(rows_dev * block_len, model_dim)
    grad_flat = grad_rows.reshape(rows_dev * block_len, head_count)
    columns = source_rows.astype(jnp.float32)
    weight_grad = lax.psum_scatter(
        lax.dot_general(columns, grad_flat, (((0,), (0,)), ((), ())), precision=HIGHEST_PRECISION),
        ("ctx", "dp"),
        scatter_dimension=0,
        tiled=True,
    )
    return (head_grad, grad_b, grad_c, weight_grad)


def mm(a, b):
    return jnp.dot(a, b, preferred_element_type=jnp.float32)


def nt(a, b, precision=None):
    return lax.dot_general(
        a, b, (((1,), (1,)), ((), ())), precision=precision, preferred_element_type=jnp.float32
    )


def one_hot(mask, kind=jnp.bfloat16):
    return jnp.where(mask, 1.0, 0.0).astype(kind)


def iotas(rows, columns):
    return (
        lax.broadcasted_iota(jnp.int32, (rows, columns), 0),
        lax.broadcasted_iota(jnp.int32, (rows, columns), 1),
    )


def eye(size, kind=jnp.bfloat16):
    row, column = iotas(size, size)
    return one_hot(row == column, kind)


def two_parts(array):
    high = array.astype(jnp.bfloat16)
    return high, (array - high.astype(jnp.float32)).astype(jnp.bfloat16)


def remote(src, dst, send_sem, recv_sem, **where):
    return pltpu.make_async_remote_copy(
        src_ref=src,
        dst_ref=dst,
        send_sem=send_sem,
        recv_sem=recv_sem,
        device_id=where,
        device_id_type=pl.DeviceIdType.MESH,
    )


def layer_kernel(
    dims,
    u_hbm, x_hbm, b_hbm, c_hbm, w_hbm, log_hbm, place_hbm, start_hbm, g_hbm,
    dx_ref, db_ref, dc_ref, dw_ref,
    u_ref, x_ref, bc_ref, log_ref, place_ref, start_ref, g_ref,
    wall, us, uall, xs, xr, bcs, bcr, raws, rawr, xp,
    step_wide, enter_wide, leave_wide, y_acc, gs_acc, eg, lx,
    end_own, back_own, f_out, f_in, g_out, g_in,
    cum_col, cum_row, step_row, gram_grad, gsl, gall, ps, pr,
    wz_s, wz_r, wx_s, wx_r, wc_s, wc_r, u_s, u_r, x_s, x_r, bc_s, bc_r, raw_s, raw_r,
    f_s, f_r, b_s, b_r, g_s, g_r, p_s, p_r, in_s,
):
    n, m, length, heads, head_dim, state, chunks = dims
    f32, bf = jnp.float32, jnp.bfloat16
    me, mine = lax.axis_index("ctx"), lax.axis_index("dp")
    rows = length // n
    block = w_hbm.shape[1]
    width = heads * head_dim
    wide = width // chunks
    per = 128 // head_dim

    def z_peer(k):
        return lax.rem(me + k, n)

    def d_peer(k):
        return lax.rem(mine + k, m)

    def piece(k):
        return pl.ds(pl.multiple_of(k * rows, rows), rows)

    barrier = pltpu.get_barrier_semaphore()
    for kz in range(n):
        for kd in range(m):
            if kz or kd:
                pl.semaphore_signal(
                    barrier, inc=1, device_id={"ctx": z_peer(kz), "dp": d_peer(kd)},
                    device_id_type=pl.DeviceIdType.MESH,
                )

    loads = [
        pltpu.make_async_copy(src, dst, in_s.at[k])
        for k, (src, dst) in enumerate(
            (
                (place_hbm, place_ref),
                (w_hbm, wall.at[mine, me]),
                (x_hbm, x_ref),
                (b_hbm, bc_ref.at[0:state]),
                (c_hbm, bc_ref.at[state : 2 * state]),
                (u_hbm, u_ref),
                (start_hbm, start_ref),
                (log_hbm, log_ref),
                (g_hbm, g_ref),
            )
        )
    ]
    for load in loads:
        load.start()
    row, column = iotas(length, length)
    row_f = row.astype(f32)
    before = one_hot(row < column)
    lower = one_hot(row >= column)

    def prefix(flags):
        return mm(jnp.broadcast_to(flags, (8, length)).astype(bf), before)[0:1]

    loads[0].wait()
    own_place = jnp.zeros((1, length), jnp.int32)
    for k in range(n):
        own_place = jnp.where(me == k, place_ref[:, k * length : (k + 1) * length], own_place)
    slot = jnp.zeros((1, length), f32)
    for k in range(n):
        flags = one_hot((own_place >= k * length) & (own_place < (k + 1) * length), f32)
        slot = slot + flags * (k * rows + prefix(flags))
    p_send = one_hot(slot == row_f)
    loads[1].wait()
    pl.semaphore_wait(barrier, n * m - 1)

    w_z = []
    for k in range(1, n):
        copy = remote(
            wall.at[mine, me], wall.at[mine, me], wz_s.at[k], wz_r.at[k], ctx=z_peer(k), dp=mine
        )
        copy.start()
        w_z.append(copy)

    other = mine + 1 - 2 * lax.rem(mine, 2)
    chips = m // 2
    w_chip, w_core = [], []

    def z_from(k):
        return lax.rem(me + n - k, n)

    def pass_on(j, k):
        held = wall.at[lax.rem(mine + m - 2 * j, m), z_from(k)]
        copy = remote(held, held, wc_s.at[j, k], wc_r.at[j, k], ctx=me, dp=other)
        copy.start()
        w_core.append(copy)

    def spread_out(k):
        for j in range(1, chips):
            held = wall.at[mine, z_from(k)]
            copy = remote(
                held, held, wx_s.at[j, k], wx_r.at[j, k], ctx=me, dp=lax.rem(mine + 2 * j, m)
            )
            copy.start()
            w_chip.append((j, k, copy))
        pass_on(0, k)

    spread_out(0)
    for load in loads[2:6]:
        load.wait()
    bcs[...] = nt(p_send, bc_ref[...]).astype(bf)
    x_copies, bc_copies = [[] for _ in range(chunks)], []

    def lanes(c):
        return slice(c * wide, (c + 1) * wide)

    def send_x(c):
        xs[c] = mm(p_send, x_ref[:, lanes(c)]).astype(bf)
        for k in range(1, n):
            to = z_peer(k)
            copy = remote(
                xs.at[c, piece(to)], xr.at[c, piece(me)], x_s.at[c, k], x_r.at[c, k],
                ctx=to, dp=mine,
            )
            copy.start()
            x_copies[c].append(copy)
        xr[c, piece(me)] = xs[c, piece(me)]

    for k in range(1, n):
        to = z_peer(k)
        copy = remote(
            bcs.at[piece(to)], bcr.at[piece(me)], bc_s.at[k], bc_r.at[k], ctx=to, dp=mine
        )
        copy.start()
        bc_copies.append(copy)
    send_x(0)
    bcr[piece(me)] = bcs[piece(me)]

    for d in range(m):
        for z in range(n):
            at = (z * m + d) * block
            us[d, :, z * block : (z + 1) * block] = mm(
                p_send, u_ref[:, at : at + block]
            ).astype(bf)
    uall[mine] = us[mine]

    p_recv = jnp.zeros((length, length), f32)
    p_back = jnp.zeros((length, length), f32)
    for k in range(n):
        place = place_ref[:, k * length : (k + 1) * length] - me * length
        here = (place >= 0) & (place < length)
        rank = jnp.where(here, k * rows + prefix(one_hot(here, f32)), -1.0)
        lands = one_hot(place == row)
        comes = one_hot(rank == row_f)
        p_recv = p_recv + nt(lands, comes)
        p_back = p_back + nt(comes, lands)
    p_recv, p_back = p_recv.astype(bf), p_back.astype(bf)

    for load in loads[6:]:
        load.wait()
    starts = jnp.broadcast_to(start_ref[...].astype(f32), (8, length)).astype(bf)
    seg_col = nt(lower, starts)[:, 0:1]
    seg_row = nt(starts, lower)[0:1]
    seg_last = seg_row[:, length - 1 : length]
    joined = (seg_col == seg_row) & (row >= column)
    joined_t = (seg_col == seg_row) & (row <= column)
    alive = one_hot(seg_col == 0.0, f32)
    tail = one_hot(seg_col == seg_last, f32)
    alive_last = one_hot(seg_last == 0.0, f32)

    for k in range(1, n):
        w_z[k - 1].wait_recv()
        spread_out(k)
    for c in range(1, chunks // 2):
        send_x(c)
    for j, k, copy in w_chip:
        copy.wait_recv()
        pass_on(j, k)
    raw = jnp.zeros((length, heads), f32)
    for core in range(2):
        if core:
            for copy in w_core:
                copy.wait_recv()
        for chip in range(chips):
            part = lax.rem(jnp.where(core, other, mine) + 2 * chip, m)
            for z in range(n):
                raw = raw + nt(us[part, :, z * block : (z + 1) * block], wall[part, z])
    raws[...] = raw.astype(bf)
    raw_copies = []
    for k in range(1, n):
        to = z_peer(k)
        copy = remote(
            raws.at[piece(to)], rawr.at[piece(me)], raw_s.at[k], raw_r.at[k], ctx=to, dp=mine
        )
        copy.start()
        raw_copies.append(copy)
    rawr[piece(me)] = raws[piece(me)]
    for c in range(chunks // 2, chunks):
        send_x(c)

    for copy in bc_copies:
        copy.wait_recv()
    both = mm(p_recv, bcr[...]).astype(bf)
    b_pack, c_pack = both[:, :state], both[:, state:]
    both_turned = nt(eye(2 * state), both).astype(bf)
    b_turn, c_turn = both_turned[:state], both_turned[state:]
    gram = nt(c_pack, b_pack)
    gram_t = nt(b_pack, c_pack)
    head_row, head_column = iotas(heads, width)
    spread = one_hot(
        (head_column >= head_row * head_dim) & (head_column < (head_row + 1) * head_dim)
    )

    def expand(array):
        high, low = two_parts(array)
        return mm(high, spread) + mm(low, spread)

    for copy in raw_copies:
        copy.wait_recv()
    u_copies = []
    for k in range(1, m):
        to = d_peer(k)
        copy = remote(us.at[to], uall.at[mine], u_s.at[k], u_r.at[k], ctx=me, dp=to)
        copy.start()
        u_copies.append(copy)
    raw_step = mm(p_recv, rawr[...])
    rate = jnp.exp(log_ref[...])
    step = jnp.maximum(raw_step, 0.0) + jnp.log1p(jnp.exp(-jnp.abs(raw_step)))
    log_decay = -step * rate
    cumul = jnp.dot(
        lower.astype(f32), log_decay, precision=HIGHEST_PRECISION, preferred_element_type=f32
    )
    total = cumul[length - 1 : length]
    decay_total = jnp.exp(total) * alive_last
    decay_wide = expand(jnp.broadcast_to(decay_total, (8, heads)))[0:1]
    step_wide[...] = expand(step)
    enter_wide[...] = expand(jnp.exp(cumul) * alive)
    leave_wide[...] = expand(jnp.exp(total - cumul) * tail)
    eg[...] = (enter_wide[...] * g_ref[...].astype(f32)).astype(bf)

    f_copies = [
        remote(f_out.at[c], f_in.at[c], f_s.at[c], f_r.at[c], ctx=lax.rem(me + 1, n), dp=mine)
        for c in range(chunks)
    ]
    b_copies = [
        remote(g_out.at[c], g_in.at[c], b_s.at[c], b_r.at[c], ctx=lax.rem(me + n - 1, n), dp=mine)
        for c in range(chunks)
    ]
    for c in range(chunks):
        back_own[c] = mm(c_turn, eg[:, lanes(c)])

        @pl.when(me == n - 1)
        def _():
            g_in[c] = jnp.zeros((state, wide), g_in.dtype)
            g_out[c] = back_own[c].astype(g_out.dtype)
            b_copies[c].start()

    eye_f = eye(heads, f32)
    cum_row[...] = nt(eye_f, cumul, HIGHEST_PRECISION)
    step_row[...] = nt(eye_f, step, HIGHEST_PRECISION)
    for k in range(heads // per):
        cum_col[k, :, 0:per] = cumul[:, k * per : (k + 1) * per]
    gram_grad[...] = jnp.zeros_like(gram_grad)
    lane_head = lax.broadcasted_iota(jnp.int32, (length, 128), 1)

    def only(array, q):
        return jnp.where(
            (lane_head >= q * head_dim) & (lane_head < (q + 1) * head_dim), array, 0.0
        ).astype(bf)

    def intra(at, _):
        here = pl.ds(pl.multiple_of(at * 128, 128), 128)
        g4 = g_ref[:, here].astype(f32)
        x4 = xp[:, here].astype(f32)
        s4 = x4 * step_wide[:, here]
        stack = lambda array: jnp.concatenate([only(array, q) for q in range(per)], axis=0)
        inner = nt(g4.astype(bf), stack(x4))
        weights, turned = [], []
        columns = cum_col[at]
        grown = gram_grad[...]
        for q in range(per):
            across = cum_row[pl.ds(at * per + q, 1), :]
            down = columns[:, q : q + 1]
            apart = down - across
            kernel = jnp.where(joined, jnp.exp(apart), 0.0)
            kernel_t = jnp.where(joined_t, jnp.exp(-apart), 0.0)
            scale = step_row[pl.ds(at * per + q, 1), :]
            grown = grown + kernel * (inner[:, q * length : (q + 1) * length] * scale)
            weights.append((kernel * gram).astype(bf))
            turned.append((kernel_t * gram_t).astype(bf))
        gram_grad[...] = grown
        y_acc[:, here] = mm(jnp.concatenate(weights, axis=1), stack(s4))
        gs_acc[:, here] = mm(jnp.concatenate(turned, axis=1), stack(g4))
        return 0

    grad_c = jnp.zeros((state, length), f32)
    grad_b = jnp.zeros((state, length), f32)
    head_sums = jnp.zeros((3 * length + 32, heads), f32)
    groups = heads // per // chunks

    def relay_forward(c):
        @pl.when(me > 0)
        def _():
            f_copies[c].wait_recv()

        @pl.when((me > 0) & (me < n - 1))
        def _():
            f_out[c] = (
                decay_wide[:, lanes(c)] * f_in[c].astype(f32) + end_own[c]
            ).astype(f_out.dtype)
            f_copies[c].start()

    def relay_back(c):
        @pl.when(me < n - 1)
        def _():
            b_copies[c].wait_recv()

        @pl.when((me > 0) & (me < n - 1))
        def _():
            g_out[c] = (
                decay_wide[:, lanes(c)] * g_in[c].astype(f32) + back_own[c]
            ).astype(g_out.dtype)
            b_copies[c].start()

    for c in range(chunks):
        for copy in x_copies[c]:
            copy.wait_recv()
        xp[:, lanes(c)] = mm(p_recv, xr[c]).astype(bf)
        lx[:, lanes(c)] = (
            leave_wide[:, lanes(c)] * step_wide[:, lanes(c)] * xp[:, lanes(c)].astype(f32)
        ).astype(bf)
        end_own[c] = mm(b_turn, lx[:, lanes(c)])

        @pl.when(me == 0)
        def _():
            f_in[c] = jnp.zeros((state, wide), f_in.dtype)
            f_out[c] = end_own[c].astype(f_out.dtype)
            f_copies[c].start()

        lax.fori_loop(c * groups, (c + 1) * groups, intra, 0)

        @pl.when(me < n // 2)
        def _():
            relay_forward(c)

        @pl.when(me >= n // 2)
        def _():
            relay_back(c)

    for c in range(chunks):

        @pl.when(me < n // 2)
        def _():
            relay_back(c)

        @pl.when(me >= n // 2)
        def _():
            relay_forward(c)

        end_all = decay_wide[:, lanes(c)] * f_in[c].astype(f32) + end_own[c]
        state_in, state_grad = f_in[c].astype(bf), g_in[c].astype(bf)
        y = y_acc[:, lanes(c)] + enter_wide[:, lanes(c)] * mm(c_pack, state_in)
        grad_scaled = gs_acc[:, lanes(c)] + leave_wide[:, lanes(c)] * mm(b_pack, state_grad)
        dx_ref[:, lanes(c)] = (grad_scaled * step_wide[:, lanes(c)]).astype(bf)
        members = spread[:, lanes(c)]

        met = jnp.sum(g_in[c].astype(f32) * end_all, axis=0, keepdims=True)
        high, low = two_parts(xp[:, lanes(c)].astype(f32) * grad_scaled)
        out_terms = (g_ref[:, lanes(c)].astype(f32) * y).astype(bf)
        terms = (out_terms, high, low, *two_parts(jnp.broadcast_to(met, (16, wide))))
        head_sums = head_sums + nt(jnp.concatenate(terms, axis=0), members)
        grad_c = grad_c + nt(state_in, eg[:, lanes(c)])
        grad_b = grad_b + nt(state_grad, lx[:, lanes(c)])

    out_sum = head_sums[:length]
    in_sum = head_sums[length : 2 * length] + head_sums[2 * length : 3 * length]
    last_extra = head_sums[3 * length : 3 * length + 8] + head_sums[
        3 * length + 16 : 3 * length + 24
    ]
    grad_cumul = out_sum - step * in_sum
    grad_log = (
        jnp.dot(
            one_hot(row <= column, f32),
            grad_cumul,
            precision=HIGHEST_PRECISION,
            preferred_element_type=f32,
        )
        + last_extra[0:1]
    )
    grad_raw = (in_sum - rate * grad_log) / (1.0 + jnp.exp(-raw_step))
    gsl[...] = mm(p_back, jnp.concatenate(two_parts(grad_raw), axis=1)).astype(bf)
    gall[mine, piece(me)] = gsl[piece(me)]
    g_copies = []
    for kz in range(n):
        for kd in range(m):
            if kz or kd:
                to = z_peer(kz)
                copy = remote(
                    gsl.at[piece(to)], gall.at[mine, piece(me)], g_s.at[kz, kd], g_r.at[kz, kd],
                    ctx=to, dp=d_peer(kd),
                )
                copy.start()
                g_copies.append(copy)

    gram_b = gram_grad[...].astype(bf)
    dc_ref[...] = grad_c + nt(b_turn, gram_b)
    db_ref[...] = grad_b + mm(c_turn, gram_b)

    for copy in u_copies:
        copy.wait_recv()
    for copy in g_copies:
        copy.wait_recv()
    eye_b = eye(2 * heads)
    turned_grads = [nt(eye_b, gall[d]).astype(bf) for d in range(m)]

    def weight_part(z):
        part = jnp.zeros((2 * heads, block), f32)
        for d in range(m):
            part = part + mm(
                turned_grads[d],
                uall[d, :, pl.ds(pl.multiple_of(z * block, block), block)],
            )
        return part[:heads] + part[heads:]

    p_copies = []
    for k in range(1, n):
        to = z_peer(k)
        ps[k] = weight_part(to).astype(ps.dtype)
        copy = remote(ps.at[k], pr.at[k], p_s.at[k], p_r.at[k], ctx=to, dp=mine)
        copy.start()
        p_copies.append(copy)
    summed = weight_part(me)
    for k, copy in enumerate(p_copies):
        copy.wait_recv()
        summed = summed + pr[k + 1].astype(f32)
    dw_ref[...] = summed

    for copy in w_z + [w[2] for w in w_chip] + w_core + u_copies + sum(x_copies, []) + bc_copies + raw_copies + g_copies + p_copies:
        copy.wait_send()
    for c in range(chunks):

        @pl.when(me < n - 1)
        def _():
            f_copies[c].wait_send()

        @pl.when(me > 0)
        def _():
            b_copies[c].wait_send()


def hand_over(*refs):
    count = len(refs) // 2
    copies = [
        pltpu.make_async_copy(refs[k], refs[count + k], refs[-1].at[k]) for k in range(count)
    ]
    for copy in copies:
        copy.start()
    for copy in copies:
        copy.wait()


def fits(n, m, rows_dev, length, heads, head_dim, state, block):
    return (
        rows_dev == 1
        and length == 128
        and (length // n) % 16 == 0
        and 128 % head_dim == 0
        and heads * head_dim % 1024 == 0
        and heads % 8 == 0
        and block % 128 == 0
        and m % 2 == 0
    )


def on_device_fused(
    layer_input,
    head_input,
    input_map,
    output_map,
    step_weight,
    decay_log,
    pack_place,
    doc_starts,
    out_grad,
):
    n, m = lax.axis_size("ctx"), lax.axis_size("dp")
    _, length, width = head_input.shape
    heads, state, model = decay_log.shape[0], input_map.shape[2], layer_input.shape[2]
    block = step_weight.shape[0]
    chunks = 4
    wide = width // chunks
    per = 128 // (width // heads)
    f32, bf = jnp.float32, jnp.bfloat16
    dims = (n, m, length, heads, width // heads, state, chunks)
    vmem, dma = pltpu.VMEM, pltpu.SemaphoreType.DMA
    whole = pl.BlockSpec(memory_space=pltpu.VMEM)
    scratch = [
        vmem((length, n * m * block), bf),
        vmem((length, width), bf),
        vmem((2 * state, length), bf),
        vmem((1, heads), f32),
        vmem((1, n * length), jnp.int32),
        vmem((1, length), jnp.int32),
        vmem((length, width), bf),
        vmem((m, n, heads, block), bf),
        vmem((m, length, n * block), bf),
        vmem((m, length, n * block), bf),
        vmem((chunks, length, wide), bf),
        vmem((chunks, length, wide), bf),
        vmem((length, 2 * state), bf),
        vmem((length, 2 * state), bf),
        vmem((length, heads), bf),
        vmem((length, heads), bf),
        vmem((length, width), bf),
        vmem((length, width), f32),
        vmem((length, width), f32),
        vmem((length, width), f32),
        vmem((length, width), f32),
        vmem((length, width), f32),
        vmem((length, width), bf),
        vmem((length, width), bf),
        vmem((chunks, state, wide), f32),
        vmem((chunks, state, wide), f32),
        vmem((chunks, state, wide), bf),
        vmem((chunks, state, wide), bf),
        vmem((chunks, state, wide), bf),
        vmem((chunks, state, wide), bf),
        vmem((heads // per, length, 128), f32),
        vmem((heads, length), f32),
        vmem((heads, length), f32),
        vmem((length, length), f32),
        vmem((length, 2 * heads), bf),
        vmem((m, length, 2 * heads), bf),
        vmem((n, heads, block), bf),
        vmem((n, heads, block), bf),
        dma((n,)), dma((n,)), dma((m // 2, n)), dma((m // 2, n)), dma((m // 2, n)), dma((m // 2, n)),
        dma((m,)), dma((m,)),
        dma((chunks, n)), dma((chunks, n)), dma((n,)), dma((n,)), dma((n,)), dma((n,)),
        dma((chunks,)), dma((chunks,)), dma((chunks,)), dma((chunks,)),
        dma((n, m)), dma((n, m)), dma((n,)), dma((n,)), dma((9,)),
    ]
    results = (
        jax.ShapeDtypeStruct((length, width), bf),
        jax.ShapeDtypeStruct((state, length), f32),
        jax.ShapeDtypeStruct((state, length), f32),
        jax.ShapeDtypeStruct((heads, block), f32),
    )
    grads = pl.pallas_call(
        functools.partial(layer_kernel, dims),
        out_shape=results,
        in_specs=[pl.BlockSpec(memory_space=pltpu.HBM)] * 9,
        out_specs=(whole,) * 4,
        scratch_shapes=scratch,
        compiler_params=pltpu.CompilerParams(
            collective_id=0, has_side_effects=True, vmem_limit_bytes=56 * 1024 * 1024
        ),
    )(
        layer_input[0],
        head_input[0],
        input_map[0].T,
        output_map[0].T,
        step_weight.T,
        decay_log[None],
        pack_place,
        doc_starts,
        out_grad[0],
    )
    head_grad, grad_b, grad_c, weight_grad = pl.pallas_call(
        hand_over,
        out_shape=results,
        in_specs=[whole] * 4,
        out_specs=(pl.BlockSpec(memory_space=pltpu.HBM),) * 4,
        scratch_shapes=[dma((4,))],
    )(*grads)
    return head_grad[None], grad_b.T[None], grad_c.T[None], weight_grad.T


def solution(mesh):
    placed = (
        P(("groups", "dp"), "ctx", None),
        P(("groups", "dp"), "ctx", None),
        P(("groups", "dp"), "ctx", None),
        P(("groups", "dp"), "ctx", None),
        P(("ctx", "dp"), None),
        P(),
        P(("groups", "dp"), None),
        P(("groups", "dp"), "ctx"),
        P(("groups", "dp"), "ctx", None),
    )

    def chosen(*arrays):
        n, m = mesh.shape["ctx"], mesh.shape["dp"]
        rows_dev, length, width = arrays[1].shape
        heads = arrays[5].shape[0]
        sizes = (rows_dev, length, heads, width // heads, arrays[2].shape[2], arrays[4].shape[0])
        return (on_device_fused if fits(n, m, *sizes) else on_device)(*arrays)

    return jax.shard_map(
        chosen,
        mesh=mesh,
        in_specs=placed,
        out_specs=(
            P(("groups", "dp"), "ctx", None),
            P(("groups", "dp"), "ctx", None),
            P(("groups", "dp"), "ctx", None),
            P(("groups", "ctx", "dp"), None),
        ),
        check_vma=False,
    )
```

```python
import functools

import jax
import jax.numpy as jnp
from jax import lax
from jax.experimental import pallas as pl
from jax.experimental.pallas import tpu as pltpu
from jax.sharding import PartitionSpec as P

HIGHEST_PRECISION = lax.Precision.HIGHEST


def carried_in(array, axis, combine, identity, reverse):
    size, mine = (lax.axis_size(axis), lax.axis_index(axis))
    everything = jax.tree.map(lambda part: lax.all_gather(part, axis), array)
    start = jax.tree.map(
        lambda part, zero: jnp.broadcast_to(jnp.asarray(zero, part.dtype), part.shape),
        array,
        identity,
    )

    def turn(k, before):
        at = size - 1 - k if reverse else k
        reached = at > mine if reverse else at < mine
        new = combine(before, jax.tree.map(lambda part: part[at], everything))
        return jax.tree.map(lambda a, b: jnp.where(reached, a, b), new, before)

    return lax.fori_loop(0, size, turn, start)


def contract(form, *operands):
    return jnp.einsum(form, *operands, precision=HIGHEST_PRECISION)


def chain_link(earlier, later):
    return (earlier[0] * later[0], later[1] + later[0][:, :, None, None] * earlier[1])


def route_slots(pack_place, block_len):
    shard_index = lax.axis_index("ctx")
    local_place = lax.dynamic_slice_in_dim(pack_place, shard_index * block_len, block_len, 1)
    sender_order = jnp.argsort(local_place, axis=1)
    targets = shard_index * block_len + jnp.arange(block_len, dtype=jnp.int32)
    all_positions = jnp.arange(pack_place.shape[1], dtype=jnp.int32)
    matches = pack_place[:, None, :] == targets[None, :, None]
    anchor = jnp.sum(jnp.where(matches, all_positions[None, None, :], 0), axis=2) // block_len
    positions = jnp.arange(block_len, dtype=jnp.int32)
    before = positions[None, :] < positions[:, None]
    same_anchor = (anchor[:, :, None] == anchor[:, None, :]) & before[None]
    rank_within = jnp.sum(same_anchor.astype(jnp.int32), axis=2)
    return (sender_order, anchor * (block_len // lax.axis_size("ctx")) + rank_within)


def on_device(
    layer_input,
    head_input,
    input_map,
    output_map,
    step_weight,
    decay_log,
    pack_place,
    doc_starts,
    out_grad,
):
    shard_count = lax.axis_size("ctx")
    rows_dev, block_len, inner_width = head_input.shape
    head_count = decay_log.shape[0]
    head_dim = inner_width // head_count
    model_dim = layer_input.shape[2]
    send_rows = block_len // shard_count
    sender_order, slot_index = route_slots(pack_place, block_len)

    def for_sending(array):
        ordered = jnp.take_along_axis(array, sender_order[:, :, None], axis=1)
        return ordered.reshape(rows_dev, shard_count, send_rows, array.shape[2])

    def packed_order(received):
        flat_rows = received.reshape(rows_dev, block_len, received.shape[3])
        return jnp.take_along_axis(flat_rows, slot_index[:, :, None], axis=1)

    flat_rows = layer_input.reshape(rows_dev * block_len, model_dim)
    columns = flat_rows
    summed = jnp.dot(
        columns,
        lax.all_gather(step_weight, ("ctx", "dp"), axis=0, tiled=True),
        preferred_element_type=jnp.float32,
    )
    raw_local = lax.optimization_barrier(summed.astype(jnp.bfloat16)).reshape(
        rows_dev, block_len, head_count
    )
    received = (
        lax.all_to_all(for_sending(head_input), "ctx", split_axis=1, concat_axis=1, tiled=True),
        lax.all_to_all(for_sending(input_map), "ctx", split_axis=1, concat_axis=1, tiled=True),
        lax.all_to_all(for_sending(output_map), "ctx", split_axis=1, concat_axis=1, tiled=True),
        lax.all_to_all(for_sending(raw_local), "ctx", split_axis=1, concat_axis=1, tiled=True),
    )
    x_packed = packed_order(received[0])
    b_packed = packed_order(received[1])
    c_packed = packed_order(received[2])
    raw_packed = packed_order(received[3])
    decay_rate = jnp.exp(decay_log)
    raw_step = raw_packed.astype(jnp.float32)
    step_size = jax.nn.softplus(raw_step)
    log_decay = -step_size * decay_rate[None, None, :]
    cumul = jnp.cumsum(log_decay, axis=1)
    segment = jnp.cumsum(doc_starts, axis=1)
    alive = (segment == 0).astype(jnp.float32)
    positions = jnp.arange(block_len, dtype=jnp.int32)
    causal = positions[:, None] >= positions[None, :]
    joined = ((segment[:, :, None] == segment[:, None, :]) & causal[None])[:, None]
    cumul_heads = jnp.transpose(cumul, (0, 2, 1))
    spread = cumul_heads[:, :, :, None] - cumul_heads[:, :, None, :]
    kernel = jnp.where(joined, jnp.exp(jnp.where(joined, spread, 0.0)), 0.0)
    x_heads = x_packed.astype(jnp.float32).reshape(rows_dev, block_len, head_count, head_dim)
    b_full = b_packed.astype(jnp.float32)
    c_full = c_packed.astype(jnp.float32)
    scaled = x_heads * step_size[:, :, :, None]
    gram = contract("rin,rjn->rij", c_full, b_full)
    weighted = kernel * gram[:, None]
    enter = jnp.exp(cumul) * alive[:, :, None]
    tail_mask = (segment == segment[:, -1:]).astype(jnp.float32)
    leave = jnp.exp(cumul[:, -1:, :] - cumul) * tail_mask[:, :, None]
    end_state = contract("rjh,rjhp,rjn->rhpn", leave, scaled, b_full)
    decay_total = jnp.exp(cumul[:, -1, :]) * alive[:, -1:]
    identity = (jnp.ones_like(decay_total), jnp.zeros_like(end_state))
    state_in = carried_in((decay_total, end_state), "ctx", chain_link, identity, False)[1]
    cotangent = out_grad.astype(jnp.float32).reshape(rows_dev, block_len, head_count, head_dim)
    local_back = contract("rih,rihp,rin->rhpn", enter, cotangent, c_full)
    state_grad = carried_in((decay_total, local_back), "ctx", chain_link, identity, True)[1]
    grad_scaled = contract("rhij,rihp->rjhp", weighted, cotangent) + contract(
        "rjh,rhpn,rjn->rjhp", leave, state_grad, b_full
    )
    grad_weighted = contract("rihp,rjhp->rhij", cotangent, scaled)
    grad_gram = jnp.sum(kernel * grad_weighted, axis=1)
    product = weighted * grad_weighted
    grad_cumul = jnp.transpose(jnp.sum(product, axis=3) - jnp.sum(product, axis=2), (0, 2, 1))
    readout = contract("rhpn,rin->rihp", state_in, c_full)
    grad_cumul = grad_cumul + enter * jnp.sum(cotangent * readout, axis=3)
    flow = contract("rjhp,rhpn,rjn->rjh", scaled, state_grad, b_full) * leave
    grad_cumul = grad_cumul - flow
    last_extra = jnp.sum(flow, axis=1) + decay_total * jnp.sum(state_grad * state_in, axis=(2, 3))
    grad_cumul = grad_cumul.at[:, -1, :].add(last_extra)
    grad_log = jnp.flip(jnp.cumsum(jnp.flip(grad_cumul, 1), axis=1), 1)
    grad_step = jnp.sum(x_heads * grad_scaled, axis=3) - decay_rate[None, None, :] * grad_log
    grad_raw = grad_step * jax.nn.sigmoid(raw_step)
    head_grad = (
        (grad_scaled * step_size[:, :, :, None])
        .reshape(rows_dev, block_len, inner_width)
        .astype(jnp.bfloat16)
    )
    grad_c = contract("rij,rjn->rin", grad_gram, b_full) + contract(
        "rih,rihp,rhpn->rin", enter, cotangent, state_in
    )
    grad_b = contract("rij,rin->rjn", grad_gram, c_full) + contract(
        "rjh,rjhp,rhpn->rjn", leave, scaled, state_grad
    )
    inverse_slot = jnp.argsort(slot_index, axis=1)
    arranged = jnp.take_along_axis(grad_raw, inverse_slot[:, :, None], axis=1).reshape(
        rows_dev, shard_count, send_rows, head_count
    )
    returned = lax.all_to_all(arranged, "ctx", split_axis=1, concat_axis=1, tiled=True).reshape(
        rows_dev, block_len, head_count
    )
    inverse_order = jnp.argsort(sender_order, axis=1)
    grad_rows = jnp.take_along_axis(returned, inverse_order[:, :, None], axis=1)
    source_rows = layer_input.reshape(rows_dev * block_len, model_dim)
    grad_flat = grad_rows.reshape(rows_dev * block_len, head_count)
    columns = source_rows.astype(jnp.float32)
    weight_grad = lax.psum_scatter(
        lax.dot_general(columns, grad_flat, (((0,), (0,)), ((), ())), precision=HIGHEST_PRECISION),
        ("ctx", "dp"),
        scatter_dimension=0,
        tiled=True,
    )
    return (head_grad, grad_b, grad_c, weight_grad)


def mm(a, b):
    return jnp.dot(a, b, preferred_element_type=jnp.float32)


def nt(a, b, precision=None):
    return lax.dot_general(
        a, b, (((1,), (1,)), ((), ())), precision=precision, preferred_element_type=jnp.float32
    )


def one_hot(mask, kind=jnp.bfloat16):
    return jnp.where(mask, 1.0, 0.0).astype(kind)


def iotas(rows, columns):
    return (
        lax.broadcasted_iota(jnp.int32, (rows, columns), 0),
        lax.broadcasted_iota(jnp.int32, (rows, columns), 1),
    )


def eye(size, kind=jnp.bfloat16):
    row, column = iotas(size, size)
    return one_hot(row == column, kind)


def two_parts(array):
    high = array.astype(jnp.bfloat16)
    return high, (array - high.astype(jnp.float32)).astype(jnp.bfloat16)


def remote(src, dst, send_sem, recv_sem, **where):
    return pltpu.make_async_remote_copy(
        src_ref=src,
        dst_ref=dst,
        send_sem=send_sem,
        recv_sem=recv_sem,
        device_id=where,
        device_id_type=pl.DeviceIdType.MESH,
    )


def layer_kernel(
    dims,
    u_hbm, x_hbm, b_hbm, c_hbm, w_hbm, log_hbm, place_hbm, start_hbm, g_hbm,
    dx_ref, db_ref, dc_ref, dw_ref,
    u_ref, x_ref, bc_ref, log_ref, place_ref, start_ref, g_ref,
    wall, us, uall, xs, xr, bcs, bcr, raws, rawr, xp,
    step_wide, enter_wide, leave_wide, y_acc, gs_acc, eg, lx,
    end_own, back_own, f_out, f_in, g_out, g_in,
    cum_col, cum_row, step_row, gram_grad, gsl, gall, ps, pr,
    wz_s, wz_r, wx_s, wx_r, wc_s, wc_r, u_s, u_r, x_s, x_r, bc_s, bc_r, raw_s, raw_r,
    f_s, f_r, b_s, b_r, g_s, g_r, p_s, p_r, in_s,
):
    n, m, length, heads, head_dim, state, chunks = dims
    f32, bf = jnp.float32, jnp.bfloat16
    me, mine = lax.axis_index("ctx"), lax.axis_index("dp")
    rows = length // n
    block = w_hbm.shape[1]
    width = heads * head_dim
    wide = width // chunks
    per = 128 // head_dim

    def z_peer(k):
        return lax.rem(me + k, n)

    def d_peer(k):
        return lax.rem(mine + k, m)

    def piece(k):
        return pl.ds(pl.multiple_of(k * rows, rows), rows)

    barrier = pltpu.get_barrier_semaphore()
    for kz in range(n):
        for kd in range(m):
            if kz or kd:
                pl.semaphore_signal(
                    barrier, inc=1, device_id={"ctx": z_peer(kz), "dp": d_peer(kd)},
                    device_id_type=pl.DeviceIdType.MESH,
                )

    loads = [
        pltpu.make_async_copy(src, dst, in_s.at[k])
        for k, (src, dst) in enumerate(
            (
                (place_hbm, place_ref),
                (w_hbm, wall.at[mine, me]),
                (x_hbm, x_ref),
                (b_hbm, bc_ref.at[0:state]),
                (c_hbm, bc_ref.at[state : 2 * state]),
                (u_hbm, u_ref),
                (start_hbm, start_ref),
                (log_hbm, log_ref),
                (g_hbm, g_ref),
            )
        )
    ]
    for load in loads:
        load.start()
    row, column = iotas(length, length)
    row_f = row.astype(f32)
    before = one_hot(row < column)
    lower = one_hot(row >= column)

    def prefix(flags):
        return mm(jnp.broadcast_to(flags, (8, length)).astype(bf), before)[0:1]

    loads[0].wait()
    own_place = jnp.zeros((1, length), jnp.int32)
    for k in range(n):
        own_place = jnp.where(me == k, place_ref[:, k * length : (k + 1) * length], own_place)
    slot = jnp.zeros((1, length), f32)
    for k in range(n):
        flags = one_hot((own_place >= k * length) & (own_place < (k + 1) * length), f32)
        slot = slot + flags * (k * rows + prefix(flags))
    p_send = one_hot(slot == row_f)
    loads[1].wait()
    pl.semaphore_wait(barrier, n * m - 1)

    w_z = []
    for k in range(1, n):
        copy = remote(
            wall.at[mine, me], wall.at[mine, me], wz_s.at[k], wz_r.at[k], ctx=z_peer(k), dp=mine
        )
        copy.start()
        w_z.append(copy)

    other = mine + 1 - 2 * lax.rem(mine, 2)
    chips = m // 2
    w_chip, w_core = [], []

    def z_from(k):
        return lax.rem(me + n - k, n)

    def pass_on(j, k):
        held = wall.at[lax.rem(mine + m - 2 * j, m), z_from(k)]
        copy = remote(held, held, wc_s.at[j, k], wc_r.at[j, k], ctx=me, dp=other)
        copy.start()
        w_core.append(copy)

    def spread_out(k):
        for j in range(1, chips):
            held = wall.at[mine, z_from(k)]
            copy = remote(
                held, held, wx_s.at[j, k], wx_r.at[j, k], ctx=me, dp=lax.rem(mine + 2 * j, m)
            )
            copy.start()
            w_chip.append((j, k, copy))
        pass_on(0, k)

    spread_out(0)
    for load in loads[2:6]:
        load.wait()
    bcs[...] = nt(p_send, bc_ref[...]).astype(bf)
    x_copies, bc_copies = [[] for _ in range(chunks)], []

    def lanes(c):
        return slice(c * wide, (c + 1) * wide)

    def send_x(c):
        xs[c] = mm(p_send, x_ref[:, lanes(c)]).astype(bf)
        for k in range(1, n):
            to = z_peer(k)
            copy = remote(
                xs.at[c, piece(to)], xr.at[c, piece(me)], x_s.at[c, k], x_r.at[c, k],
                ctx=to, dp=mine,
            )
            copy.start()
            x_copies[c].append(copy)
        xr[c, piece(me)] = xs[c, piece(me)]

    for k in range(1, n):
        to = z_peer(k)
        copy = remote(
            bcs.at[piece(to)], bcr.at[piece(me)], bc_s.at[k], bc_r.at[k], ctx=to, dp=mine
        )
        copy.start()
        bc_copies.append(copy)
    send_x(0)
    bcr[piece(me)] = bcs[piece(me)]

    for d in range(m):
        for z in range(n):
            at = (z * m + d) * block
            us[d, :, z * block : (z + 1) * block] = mm(
                p_send, u_ref[:, at : at + block]
            ).astype(bf)
    uall[mine] = us[mine]

    p_recv = jnp.zeros((length, length), f32)
    p_back = jnp.zeros((length, length), f32)
    for k in range(n):
        place = place_ref[:, k * length : (k + 1) * length] - me * length
        here = (place >= 0) & (place < length)
        rank = jnp.where(here, k * rows + prefix(one_hot(here, f32)), -1.0)
        lands = one_hot(place == row)
        comes = one_hot(rank == row_f)
        p_recv = p_recv + nt(lands, comes)
        p_back = p_back + nt(comes, lands)
    p_recv, p_back = p_recv.astype(bf), p_back.astype(bf)

    for load in loads[6:]:
        load.wait()
    starts = jnp.broadcast_to(start_ref[...].astype(f32), (8, length)).astype(bf)
    seg_col = nt(lower, starts)[:, 0:1]
    seg_row = nt(starts, lower)[0:1]
    seg_last = seg_row[:, length - 1 : length]
    joined = (seg_col == seg_row) & (row >= column)
    joined_t = (seg_col == seg_row) & (row <= column)
    alive = one_hot(seg_col == 0.0, f32)
    tail = one_hot(seg_col == seg_last, f32)
    alive_last = one_hot(seg_last == 0.0, f32)

    for k in range(1, n):
        w_z[k - 1].wait_recv()
        spread_out(k)
    for c in range(1, chunks // 2):
        send_x(c)
    for j, k, copy in w_chip:
        copy.wait_recv()
        pass_on(j, k)
    raw = jnp.zeros((length, heads), f32)
    for core in range(2):
        if core:
            for copy in w_core:
                copy.wait_recv()
        for chip in range(chips):
            part = lax.rem(jnp.where(core, other, mine) + 2 * chip, m)
            for z in range(n):
                raw = raw + nt(us[part, :, z * block : (z + 1) * block], wall[part, z])
    raws[...] = raw.astype(bf)
    raw_copies = []
    for k in range(1, n):
        to = z_peer(k)
        copy = remote(
            raws.at[piece(to)], rawr.at[piece(me)], raw_s.at[k], raw_r.at[k], ctx=to, dp=mine
        )
        copy.start()
        raw_copies.append(copy)
    rawr[piece(me)] = raws[piece(me)]
    for c in range(chunks // 2, chunks):
        send_x(c)

    for copy in bc_copies:
        copy.wait_recv()
    both = mm(p_recv, bcr[...]).astype(bf)
    b_pack, c_pack = both[:, :state], both[:, state:]
    both_turned = nt(eye(2 * state), both).astype(bf)
    b_turn, c_turn = both_turned[:state], both_turned[state:]
    gram = nt(c_pack, b_pack)
    gram_t = nt(b_pack, c_pack)
    head_row, head_column = iotas(heads, width)
    spread = one_hot(
        (head_column >= head_row * head_dim) & (head_column < (head_row + 1) * head_dim)
    )

    def expand(array):
        high, low = two_parts(array)
        return mm(high, spread) + mm(low, spread)

    for copy in raw_copies:
        copy.wait_recv()
    u_copies = []
    for k in range(1, m):
        to = d_peer(k)
        copy = remote(us.at[to], uall.at[mine], u_s.at[k], u_r.at[k], ctx=me, dp=to)
        copy.start()
        u_copies.append(copy)
    raw_step = mm(p_recv, rawr[...])
    rate = jnp.exp(log_ref[...])
    step = jnp.maximum(raw_step, 0.0) + jnp.log1p(jnp.exp(-jnp.abs(raw_step)))
    log_decay = -step * rate
    cumul = jnp.dot(
        lower.astype(f32), log_decay, precision=HIGHEST_PRECISION, preferred_element_type=f32
    )
    total = cumul[length - 1 : length]
    decay_total = jnp.exp(total) * alive_last
    decay_wide = expand(jnp.broadcast_to(decay_total, (8, heads)))[0:1]
    step_wide[...] = expand(step)
    enter_wide[...] = expand(jnp.exp(cumul) * alive)
    leave_wide[...] = expand(jnp.exp(total - cumul) * tail)

    f_copies = [
        remote(f_out.at[c], f_in.at[c], f_s.at[c], f_r.at[c], ctx=lax.rem(me + 1, n), dp=mine)
        for c in range(chunks)
    ]
    b_copies = [
        remote(g_out.at[c], g_in.at[c], b_s.at[c], b_r.at[c], ctx=lax.rem(me + n - 1, n), dp=mine)
        for c in range(chunks)
    ]
    for c in range(chunks):
        eg[:, lanes(c)], low = two_parts(
            enter_wide[:, lanes(c)] * g_ref[:, lanes(c)].astype(f32)
        )
        back_own[c] = mm(c_turn, eg[:, lanes(c)]) + mm(c_turn, low)

        @pl.when(me == n - 1)
        def _():
            g_in[c] = jnp.zeros((state, wide), g_in.dtype)
            g_out[c] = back_own[c].astype(g_out.dtype)
            b_copies[c].start()

    eye_f = eye(heads, f32)
    cum_row[...] = nt(eye_f, cumul, HIGHEST_PRECISION)
    step_row[...] = nt(eye_f, step, HIGHEST_PRECISION)
    for k in range(heads // per):
        cum_col[k, :, 0:per] = cumul[:, k * per : (k + 1) * per]
    gram_grad[...] = jnp.zeros_like(gram_grad)
    lane_head = lax.broadcasted_iota(jnp.int32, (length, 128), 1)

    def only(array, q):
        return jnp.where(
            (lane_head >= q * head_dim) & (lane_head < (q + 1) * head_dim), array, 0.0
        ).astype(bf)

    def intra(at, _):
        here = pl.ds(pl.multiple_of(at * 128, 128), 128)
        g4 = g_ref[:, here].astype(f32)
        x4 = xp[:, here].astype(f32)
        s4 = x4 * step_wide[:, here]
        stack = lambda array: jnp.concatenate([only(array, q) for q in range(per)], axis=0)
        inner = nt(g4.astype(bf), stack(x4))
        weights, turned = [], []
        columns = cum_col[at]
        grown = gram_grad[...]
        for q in range(per):
            across = cum_row[pl.ds(at * per + q, 1), :]
            down = columns[:, q : q + 1]
            apart = down - across
            kernel = jnp.where(joined, jnp.exp(apart), 0.0)
            kernel_t = jnp.where(joined_t, jnp.exp(-apart), 0.0)
            scale = step_row[pl.ds(at * per + q, 1), :]
            grown = grown + kernel * (inner[:, q * length : (q + 1) * length] * scale)
            weights.append((kernel * gram).astype(bf))
            turned.append((kernel_t * gram_t).astype(bf))
        gram_grad[...] = grown
        y_acc[:, here] = mm(jnp.concatenate(weights, axis=1), stack(s4))
        gs_acc[:, here] = mm(jnp.concatenate(turned, axis=1), stack(g4))
        return 0

    grad_c = jnp.zeros((state, length), f32)
    grad_b = jnp.zeros((state, length), f32)
    head_sums = jnp.zeros((3 * length + 32, heads), f32)
    groups = heads // per // chunks

    def relay_forward(c):
        @pl.when(me > 0)
        def _():
            f_copies[c].wait_recv()

        @pl.when((me > 0) & (me < n - 1))
        def _():
            f_out[c] = (
                decay_wide[:, lanes(c)] * f_in[c].astype(f32) + end_own[c]
            ).astype(f_out.dtype)
            f_copies[c].start()

    def relay_back(c):
        @pl.when(me < n - 1)
        def _():
            b_copies[c].wait_recv()

        @pl.when((me > 0) & (me < n - 1))
        def _():
            g_out[c] = (
                decay_wide[:, lanes(c)] * g_in[c].astype(f32) + back_own[c]
            ).astype(g_out.dtype)
            b_copies[c].start()

    for c in range(chunks):
        for copy in x_copies[c]:
            copy.wait_recv()
        xp[:, lanes(c)] = mm(p_recv, xr[c]).astype(bf)
        lx[:, lanes(c)], low = two_parts(
            leave_wide[:, lanes(c)] * step_wide[:, lanes(c)] * xp[:, lanes(c)].astype(f32)
        )
        end_own[c] = mm(b_turn, lx[:, lanes(c)]) + mm(b_turn, low)

        @pl.when(me == 0)
        def _():
            f_in[c] = jnp.zeros((state, wide), f_in.dtype)
            f_out[c] = end_own[c].astype(f_out.dtype)
            f_copies[c].start()

        lax.fori_loop(c * groups, (c + 1) * groups, intra, 0)

        @pl.when(me < n // 2)
        def _():
            relay_forward(c)

        @pl.when(me >= n // 2)
        def _():
            relay_back(c)

    for c in range(chunks):

        @pl.when(me < n // 2)
        def _():
            relay_back(c)

        @pl.when(me >= n // 2)
        def _():
            relay_forward(c)

        end_all = decay_wide[:, lanes(c)] * f_in[c].astype(f32) + end_own[c]
        state_in, state_grad = f_in[c].astype(bf), g_in[c].astype(bf)
        y = y_acc[:, lanes(c)] + enter_wide[:, lanes(c)] * mm(c_pack, state_in)
        grad_scaled = gs_acc[:, lanes(c)] + leave_wide[:, lanes(c)] * mm(b_pack, state_grad)
        dx_ref[:, lanes(c)] = (grad_scaled * step_wide[:, lanes(c)]).astype(bf)
        members = spread[:, lanes(c)]

        met = jnp.sum(g_in[c].astype(f32) * end_all, axis=0, keepdims=True)
        high, low = two_parts(xp[:, lanes(c)].astype(f32) * grad_scaled)
        out_terms = (g_ref[:, lanes(c)].astype(f32) * y).astype(bf)
        terms = (out_terms, high, low, *two_parts(jnp.broadcast_to(met, (16, wide))))
        head_sums = head_sums + nt(jnp.concatenate(terms, axis=0), members)
        grad_c = grad_c + nt(state_in, eg[:, lanes(c)])
        grad_b = grad_b + nt(state_grad, lx[:, lanes(c)])

    out_sum = head_sums[:length]
    in_sum = head_sums[length : 2 * length] + head_sums[2 * length : 3 * length]
    last_extra = head_sums[3 * length : 3 * length + 8] + head_sums[
        3 * length + 16 : 3 * length + 24
    ]
    grad_cumul = out_sum - step * in_sum
    grad_log = (
        jnp.dot(
            one_hot(row <= column, f32),
            grad_cumul,
            precision=HIGHEST_PRECISION,
            preferred_element_type=f32,
        )
        + last_extra[0:1]
    )
    grad_raw = (in_sum - rate * grad_log) / (1.0 + jnp.exp(-raw_step))
    gsl[...] = mm(p_back, jnp.concatenate(two_parts(grad_raw), axis=1)).astype(bf)
    gall[mine, piece(me)] = gsl[piece(me)]
    g_copies = []
    for kz in range(n):
        for kd in range(m):
            if kz or kd:
                to = z_peer(kz)
                copy = remote(
                    gsl.at[piece(to)], gall.at[mine, piece(me)], g_s.at[kz, kd], g_r.at[kz, kd],
                    ctx=to, dp=d_peer(kd),
                )
                copy.start()
                g_copies.append(copy)

    gram_b = gram_grad[...].astype(bf)
    dc_ref[...] = grad_c + nt(b_turn, gram_b)
    db_ref[...] = grad_b + mm(c_turn, gram_b)

    for copy in u_copies:
        copy.wait_recv()
    for copy in g_copies:
        copy.wait_recv()
    eye_b = eye(2 * heads)
    turned_grads = [
        jnp.concatenate([nt(eye_b, gall[d + e]).astype(bf) for e in range(2)], axis=1)
        for d in range(0, m, 2)
    ]

    def weight_part(z):
        part = jnp.zeros((2 * heads, block), f32)
        here = pl.ds(pl.multiple_of(z * block, block), block)
        for d in range(0, m, 2):
            part = part + mm(
                turned_grads[d // 2], jnp.concatenate([uall[d, :, here], uall[d + 1, :, here]], axis=0)
            )
        return part[:heads] + part[heads:]

    p_copies = []
    for k in range(1, n):
        to = z_peer(k)
        ps[k] = weight_part(to).astype(ps.dtype)
        copy = remote(ps.at[k], pr.at[k], p_s.at[k], p_r.at[k], ctx=to, dp=mine)
        copy.start()
        p_copies.append(copy)
    summed = weight_part(me)
    for k, copy in enumerate(p_copies):
        copy.wait_recv()
        summed = summed + pr[k + 1].astype(f32)
    dw_ref[...] = summed

    for copy in w_z + [w[2] for w in w_chip] + w_core + u_copies + sum(x_copies, []) + bc_copies + raw_copies + g_copies + p_copies:
        copy.wait_send()
    for c in range(chunks):

        @pl.when(me < n - 1)
        def _():
            f_copies[c].wait_send()

        @pl.when(me > 0)
        def _():
            b_copies[c].wait_send()


def hand_over(*refs):
    count = len(refs) // 2
    copies = [
        pltpu.make_async_copy(refs[k], refs[count + k], refs[-1].at[k]) for k in range(count)
    ]
    for copy in copies:
        copy.start()
    for copy in copies:
        copy.wait()


def fits(n, m, rows_dev, length, heads, head_dim, state, block):
    return (
        rows_dev == 1
        and length == 128
        and (length // n) % 16 == 0
        and 128 % head_dim == 0
        and heads * head_dim % 1024 == 0
        and heads % 8 == 0
        and block % 128 == 0
        and m % 2 == 0
    )


def on_device_fused(
    layer_input,
    head_input,
    input_map,
    output_map,
    step_weight,
    decay_log,
    pack_place,
    doc_starts,
    out_grad,
):
    n, m = lax.axis_size("ctx"), lax.axis_size("dp")
    _, length, width = head_input.shape
    heads, state, model = decay_log.shape[0], input_map.shape[2], layer_input.shape[2]
    block = step_weight.shape[0]
    chunks = 4
    wide = width // chunks
    per = 128 // (width // heads)
    f32, bf = jnp.float32, jnp.bfloat16
    dims = (n, m, length, heads, width // heads, state, chunks)
    vmem, dma = pltpu.VMEM, pltpu.SemaphoreType.DMA
    whole = pl.BlockSpec(memory_space=pltpu.VMEM)
    scratch = [
        vmem((length, n * m * block), bf),
        vmem((length, width), bf),
        vmem((2 * state, length), bf),
        vmem((1, heads), f32),
        vmem((1, n * length), jnp.int32),
        vmem((1, length), jnp.int32),
        vmem((length, width), bf),
        vmem((m, n, heads, block), bf),
        vmem((m, length, n * block), bf),
        vmem((m, length, n * block), bf),
        vmem((chunks, length, wide), bf),
        vmem((chunks, length, wide), bf),
        vmem((length, 2 * state), bf),
        vmem((length, 2 * state), bf),
        vmem((length, heads), bf),
        vmem((length, heads), bf),
        vmem((length, width), bf),
        vmem((length, width), f32),
        vmem((length, width), f32),
        vmem((length, width), f32),
        vmem((length, width), f32),
        vmem((length, width), f32),
        vmem((length, width), bf),
        vmem((length, width), bf),
        vmem((chunks, state, wide), f32),
        vmem((chunks, state, wide), f32),
        vmem((chunks, state, wide), bf),
        vmem((chunks, state, wide), bf),
        vmem((chunks, state, wide), bf),
        vmem((chunks, state, wide), bf),
        vmem((heads // per, length, 128), f32),
        vmem((heads, length), f32),
        vmem((heads, length), f32),
        vmem((length, length), f32),
        vmem((length, 2 * heads), bf),
        vmem((m, length, 2 * heads), bf),
        vmem((n, heads, block), bf),
        vmem((n, heads, block), bf),
        dma((n,)), dma((n,)), dma((m // 2, n)), dma((m // 2, n)), dma((m // 2, n)), dma((m // 2, n)),
        dma((m,)), dma((m,)),
        dma((chunks, n)), dma((chunks, n)), dma((n,)), dma((n,)), dma((n,)), dma((n,)),
        dma((chunks,)), dma((chunks,)), dma((chunks,)), dma((chunks,)),
        dma((n, m)), dma((n, m)), dma((n,)), dma((n,)), dma((9,)),
    ]
    results = (
        jax.ShapeDtypeStruct((length, width), bf),
        jax.ShapeDtypeStruct((state, length), f32),
        jax.ShapeDtypeStruct((state, length), f32),
        jax.ShapeDtypeStruct((heads, block), f32),
    )
    grads = pl.pallas_call(
        functools.partial(layer_kernel, dims),
        out_shape=results,
        in_specs=[pl.BlockSpec(memory_space=pltpu.HBM)] * 9,
        out_specs=(whole,) * 4,
        scratch_shapes=scratch,
        compiler_params=pltpu.CompilerParams(
            collective_id=0, has_side_effects=True, vmem_limit_bytes=56 * 1024 * 1024
        ),
    )(
        layer_input[0],
        head_input[0],
        input_map[0].T,
        output_map[0].T,
        step_weight.T,
        decay_log[None],
        pack_place,
        doc_starts,
        out_grad[0],
    )
    head_grad, grad_b, grad_c, weight_grad = pl.pallas_call(
        hand_over,
        out_shape=results,
        in_specs=[whole] * 4,
        out_specs=(pl.BlockSpec(memory_space=pltpu.HBM),) * 4,
        scratch_shapes=[dma((4,))],
    )(*grads)
    return head_grad[None], grad_b.T[None], grad_c.T[None], weight_grad.T


def solution(mesh):
    placed = (
        P(("groups", "dp"), "ctx", None),
        P(("groups", "dp"), "ctx", None),
        P(("groups", "dp"), "ctx", None),
        P(("groups", "dp"), "ctx", None),
        P(("ctx", "dp"), None),
        P(),
        P(("groups", "dp"), None),
        P(("groups", "dp"), "ctx"),
        P(("groups", "dp"), "ctx", None),
    )

    def chosen(*arrays):
        n, m = mesh.shape["ctx"], mesh.shape["dp"]
        rows_dev, length, width = arrays[1].shape
        heads = arrays[5].shape[0]
        sizes = (rows_dev, length, heads, width // heads, arrays[2].shape[2], arrays[4].shape[0])
        return (on_device_fused if fits(n, m, *sizes) else on_device)(*arrays)

    return jax.shard_map(
        chosen,
        mesh=mesh,
        in_specs=placed,
        out_specs=(
            P(("groups", "dp"), "ctx", None),
            P(("groups", "dp"), "ctx", None),
            P(("groups", "dp"), "ctx", None),
            P(("groups", "ctx", "dp"), None),
        ),
        check_vma=False,
    )
```
